32 devices in a mesh: groups: 2 (over y), fam: 4 (over z), trait: 2 (over x), rep: 2 (over core).
Axes of the slice: x: 2, y: 2, z: 4, core: 2. Of those that a mesh axis runs over, the one named last changes fastest.
Arguments:
- pheno: float32 [4096, 1024], P(('groups', 'fam'), 'trait'), parts along dimension 0, may hold values from -6 to 6
- match: int32 [4096], P(('groups', 'fam')), parts along dimension 0, may hold values from 0 to 2047, as said below
- diag_var: float32 [4096], P(('groups', 'fam')), parts along dimension 0, may hold values from 0.5 to 1.5
- tiles: float32 [256, 4096], P(('groups', 'fam', 'rep')), parts along dimension 0, may hold values from -0.375 to 0.375
- tile_row_family: int32 [256], P(('groups', 'fam', 'rep')), parts along dimension 0, may hold values from 0 to 7, as said below
- tile_cols: int32 [256], P(('groups', 'fam', 'rep')), parts along dimension 0, may hold values from 0 to 7
- rel_row: int32 [2048], P(('groups', 'fam', 'rep')), parts along dimension 0, may hold values from 0 to 511
- rel_peer: int32 [2048, 1], P(('groups', 'fam', 'rep')), parts along dimension 0, may hold values from 0 to 3; in each aligned block of 128 rows (0 to 127, 128 to 255, ...) at most 64 rows name the same one
- rel_slot: int32 [2048], P(('groups', 'fam', 'rep')), parts along dimension 0, may hold values from 0 to 511
- rel_weight: float32 [2048], P(('groups', 'fam', 'rep')), parts along dimension 0, may hold values from -4 to 4
Outputs:
- solution_field: float32 [4096, 1024], P(('groups', 'fam'), 'trait'), parts along dimension 0
- residual: float32 [4096, 1024], P(('groups', 'fam'), 'trait'), parts along dimension 0
The draws below stay inside these ranges and needn't reach their ends.
There are 2 independent parts, one for each index of `groups`. The reference program is written for one: setup_inputs(seed, part) draws one part's arguments, and reference() takes and returns one part's arrays. A program takes and returns all parts, laid end to end along the dimension named above; each array names one. Nothing has to cross between parts.
Inputs may be any that keep to these rules, and one draw needn't show every extreme that they name: match is a permutation of the persons; the rows of one trait-file shard (one index of fam) name at most 256 persons of one owner, and exactly 256 of some owner. The tiles of one owner sit at distinct block positions (tile_row_family, tile_cols), and every diagonal block position of the owner is among them. `rel_peer`: among the rows of one device no owner is named more than 64 times.
All inputs are finite; a program needn't handle non-finite values.
Results may differ from the reference program's by a relative error of at most 0.0003.
Values sent between devices are 32-bit elements; how exact they have to be, the bound alone decides.
A program may use at most 64 MiB of HBM per device.

```python
import math
import jax
import jax.numpy as jnp
import numpy as np
from jax import lax

TRAITS = 1024
P_DEV = 512
TILE_DEV = 16
REL_DEV = 128
ITERS = 3
PERSONS = 2048
NBLK = 8
CAPR = 64
N_FAM = 4
N_REP = 2


def tile_layout(key):
    count = N_REP * TILE_DEV
    spots = NBLK * NBLK
    keys = jax.random.split(jax.random.fold_in(key, 29), 2 * N_FAM)

    def one_owner(key_perm, key_order):
        perm = jax.random.permutation(key_perm, spots).astype(jnp.int32)
        ranking = jnp.zeros((spots,), jnp.int32).at[perm].set(jnp.arange(spots, dtype=jnp.int32))
        spot_ids = jnp.arange(spots, dtype=jnp.int32)
        offdiag = (spot_ids // NBLK != spot_ids % NBLK).astype(jnp.int32)
        score = offdiag * spots + ranking
        chosen = jnp.argsort(score, stable=True)[:count].astype(jnp.int32)
        order = jax.random.permutation(key_order, count)
        return chosen[order]
    selected_entries = jax.vmap(one_owner)(keys[:N_FAM], keys[N_FAM:]).reshape(-1)
    return (selected_entries // NBLK, selected_entries % NBLK)


def draw_tile_row_family(key, part):
    rows_out, cols_out = tile_layout(key)
    return rows_out.astype(jnp.int32)


def draw_tile_cols(key, part):
    rows_out, cols_out = tile_layout(key)
    return cols_out.astype(jnp.int32)


def draw_match(key, part):
    key = jax.random.fold_in(key, 11)
    key_amount, key_order, key_rows, key_slots = jax.random.split(key, 4)
    base = P_DEV // N_FAM
    amounts = jax.random.randint(key_amount, (N_FAM // 2,), 0, base + 1).astype(jnp.int32)
    amounts = amounts.at[0].set(base)
    signed = jnp.stack([amounts, -amounts], axis=1).reshape(N_FAM)
    order = jax.random.permutation(key_order, N_FAM)
    offsets = signed[order]
    shard_ids = jnp.arange(N_FAM, dtype=jnp.int32)[:, None]
    owner_ids = jnp.arange(N_FAM, dtype=jnp.int32)[None, :]
    counts = base + offsets[(owner_ids - shard_ids) % N_FAM]
    col_end = jnp.cumsum(counts, axis=0)
    col_start = col_end - counts
    slot_ids = jnp.arange(P_DEV, dtype=jnp.int32)
    source = jnp.sum((slot_ids[None, None, :] >= col_end[:, :, None]).astype(jnp.int32), axis=0)
    rank = slot_ids[None, :] - jnp.take_along_axis(col_start.T, source, axis=1)
    row_start = jnp.cumsum(counts, axis=1) - counts
    position = jnp.take_along_axis(row_start.T, source, axis=1) + rank
    partition_permutation = jax.vmap(lambda k: jax.random.permutation(k, P_DEV))(jax.random.split(key_rows, N_FAM))
    owner_perm = jax.vmap(lambda k: jax.random.permutation(k, P_DEV))(jax.random.split(key_slots, N_FAM))
    file_row = source * P_DEV + partition_permutation[source, position]
    person = jnp.arange(N_FAM, dtype=jnp.int32)[:, None] * P_DEV + owner_perm.astype(jnp.int32)
    match = jnp.zeros((N_FAM * P_DEV,), jnp.int32).at[file_row.reshape(-1)].set(person.reshape(-1))
    return match


def touch_ends(drawn, stream_key, least, high):
    index_at = [jax.random.randint(jax.random.fold_in(stream_key, axis), (), 0, length) for axis, length in enumerate(drawn.shape)]
    longest = drawn.shape.index(max(drawn.shape))
    next_to = index_at[:longest] + [(index_at[longest] + 1) % drawn.shape[longest]] + index_at[longest + 1:]
    return drawn.at[tuple(index_at)].set(least).at[tuple(next_to)].set(high)


def block_levels(stream_key, extent, cuts, low, high):
    def one(dim, parts):
        heights = jax.random.uniform(jax.random.fold_in(jax.random.fold_in(stream_key, 6), dim), (parts,), jnp.float32, low / len(cuts), high / len(cuts))
        return jnp.repeat(jnp.exp(heights), extent[dim] // parts).reshape((-1,) + (1,) * (len(extent) - dim - 1))

    level = one(*cuts[0])
    for cut in cuts[1:]:
        level = level * one(*cut)
    return level


def assign_block(own_key, own, number, rows, number_of, top, bound, lean):
    order = jax.random.permutation(own_key, number_of)
    packed, ordinary = shares(number_of, rows * top, bound, lean, True), shares(number_of, rows * top, bound, lean, False)
    places = jnp.arange(number_of)

    def named(sizes, offset_by):
        used = int((sizes > 0).sum())
        fixed = max(1, used // 4)
        moved = fixed + (places - fixed + offset_by * (used - fixed)) % max(1, number_of - fixed)
        return jnp.zeros((number_of,), jnp.int32).at[order[jnp.where(places < fixed, places, moved)]].set(jnp.asarray(sizes, jnp.int32))

    sizes = jnp.where(number % 4 == 0, named(packed, number // 4), named(ordinary, number - number // 4 - 1))
    mixed = jax.random.permutation(jax.random.fold_in(own, 3), number_of)
    source_of, sink = mixed[0:number_of // 2 * 2:2], mixed[1:number_of // 2 * 2:2]
    room = jnp.minimum(sizes[source_of] - 1, bound - sizes[sink]) // 2
    room = jnp.where((source_of == order[0]) | (sink == order[0]) | (sizes[sink] == 0), 0, jnp.maximum(room, 0))
    moved = jax.random.randint(jax.random.fold_in(own, 4), (number_of // 2,), 0, 1 << 20) % (room + 1)
    sizes = sizes.at[source_of].add(-moved).at[sink].add(moved)
    members = jnp.searchsorted(jnp.cumsum(sizes), jnp.arange(rows * top), side="right").astype(jnp.int32)
    listing = members.reshape(top, rows).T
    listing = listing[jax.random.permutation(jax.random.fold_in(own, 1), rows)]
    offset_by = jax.random.randint(jax.random.fold_in(own, 2), (rows, 1), 0, top)
    return jnp.take_along_axis(listing, (jnp.arange(top)[None, :] + offset_by) % top, axis=1)


def shares(count, total, most, skew, full):
    loads = [(1 << 20) // math.isqrt(grade ** skew) + 1 for grade in range(1, count + 1)]
    largest = most if full else min(most, max(-(-total // count), total * loads[0] // sum(loads)))
    least = 1 if total - largest >= count - 1 else 0
    holding, spare = [largest] + [least] * (count - 1), total - largest - least * (count - 1)
    while spare > 0:
        movable = [i for i in range(1, count) if holding[i] < largest] or [i for i in range(1, count) if holding[i] < most]
        pool, budget = sum([loads[i] for i in movable]), spare
        for i in movable:
            more = min(most - holding[i], max(1, budget * loads[i] // pool), spare)
            holding[i] = holding[i] + more
            spare = spare - more
    return np.array(holding)


def normal_values(stream_key, extent, deviation, most, cuts=(), kind=jnp.bfloat16):
    values = jax.random.normal(stream_key, extent, jnp.float32) * deviation
    if len(cuts) > 0:
        values = block_levels(stream_key, extent, cuts, -0.22, 0.18) * values
    return jnp.clip(values, min=-most, max=most).astype(kind)


def setup_inputs(seed: int = 0, part: int = 0) -> dict:
    splits = jax.random.split(jax.random.key(seed), 11)
    own_keys = jax.random.split(jax.random.fold_in(splits[10], part), 11)
    pheno = normal_values(own_keys[0], (PERSONS, TRAITS), 1.0, 6.0, ((0, 4), (1, 2)), jnp.float32)
    match = draw_match(jax.random.fold_in(jax.random.fold_in(splits[10], part), 71), part)
    diag_var = jnp.clip(0.5 + 1.0 * jax.random.uniform(own_keys[2], (PERSONS,), jnp.float32) ** block_levels(own_keys[2], (PERSONS,), ((0, 4),), -0.2, 0.2), 0.5, 1.5)
    tiles = normal_values(own_keys[3], (N_FAM * N_REP * TILE_DEV, 4096), (N_REP * TILE_DEV * 4096 // P_DEV) ** -0.5, 0.375, ((0, 8),), jnp.float32)
    tile_row_family = draw_tile_row_family(jax.random.fold_in(jax.random.fold_in(splits[10], part), 71), part)
    tile_cols = draw_tile_cols(jax.random.fold_in(jax.random.fold_in(splits[10], part), 71), part)
    rel_row = touch_ends(jax.random.randint(own_keys[6], (N_FAM * N_REP * REL_DEV,), 0, P_DEV), jax.random.fold_in(own_keys[6], 1), 0, P_DEV - 1).astype(jnp.int32)
    rel_peer_keys = jax.random.split(jax.random.fold_in(own_keys[7], 1), (N_FAM * N_REP * REL_DEV) // REL_DEV)
    rel_peer_turns = jax.random.permutation(jax.random.fold_in(own_keys[7], 3), (N_FAM * N_REP * REL_DEV) // REL_DEV)
    rel_peer = jax.vmap(lambda own, number: assign_block(jax.random.fold_in(own_keys[7], 2), own, number, REL_DEV, N_FAM, 1, CAPR, 2))(rel_peer_keys, rel_peer_turns).reshape((N_FAM * N_REP * REL_DEV, 1))
    rel_slot = touch_ends(jax.random.randint(own_keys[8], (N_FAM * N_REP * REL_DEV,), 0, P_DEV), jax.random.fold_in(own_keys[8], 1), 0, P_DEV - 1).astype(jnp.int32)
    rel_weight = normal_values(own_keys[9], (N_FAM * N_REP * REL_DEV,), 0.7, 4.0, ((0, 8),), jnp.float32)
    return {"pheno": pheno, "match": match, "diag_var": diag_var, "tiles": tiles, "tile_row_family": tile_row_family, "tile_cols": tile_cols, "rel_row": rel_row, "rel_peer": rel_peer, "rel_slot": rel_slot, "rel_weight": rel_weight}


PRECISION_HIGH = lax.Precision.HIGHEST


def owner_forward(args):
    solution_values, tiles, trow, tcol = args
    blocks = solution_values.reshape(NBLK, 64, solution_values.shape[1])
    selected_entries = blocks[tcol]
    operator_products = jnp.einsum("olh,ohj->olj", tiles, selected_entries, precision=PRECISION_HIGH)
    marker_flags = (trow[None, :] == jnp.arange(NBLK, dtype=jnp.int32)[:, None]).astype(jnp.float32)
    return jnp.einsum("fo,ouh->fuh", marker_flags, operator_products, precision=PRECISION_HIGH).reshape(solution_values.shape)


def owner_backward(args):
    solution_values, tiles, trow, tcol = args
    blocks = solution_values.reshape(NBLK, 64, solution_values.shape[1])
    selected_entries = blocks[trow]
    operator_products = jnp.einsum("zxp,zxm->zpm", tiles, selected_entries, precision=PRECISION_HIGH)
    marker_flags = (tcol[None, :] == jnp.arange(NBLK, dtype=jnp.int32)[:, None]).astype(jnp.float32)
    return jnp.einsum("fo,ouh->fuh", marker_flags, operator_products, precision=PRECISION_HIGH).reshape(solution_values.shape)


def reference(pheno, match, diag_var, tiles, tile_row_family, tile_cols, rel_row, rel_peer, rel_slot, rel_weight):
    target = jnp.zeros((PERSONS, TRAITS), jnp.float32).at[match].set(pheno)
    owner_tiles = tiles.reshape(N_FAM, N_REP * TILE_DEV, 64, 64)
    owner_rows = tile_row_family.reshape(N_FAM, N_REP * TILE_DEV)
    owner_cols = tile_cols.reshape(N_FAM, N_REP * TILE_DEV)
    entry_owner = jnp.arange(N_FAM * N_REP * REL_DEV, dtype=jnp.int32) // (N_REP * REL_DEV)
    rows_all = entry_owner * P_DEV + rel_row
    cols_all = rel_peer[:, 0] * P_DEV + rel_slot
    weights = rel_weight[:, None]

    def apply_operator(solution_values):
        split = solution_values.reshape(N_FAM, P_DEV, TRAITS)
        factor = lax.map(owner_forward, (split, owner_tiles, owner_rows, owner_cols)).reshape(PERSONS, TRAITS)
        factor = factor.at[rows_all].add(weights * solution_values[cols_all])
        split_factor = factor.reshape(N_FAM, P_DEV, TRAITS)
        back = lax.map(owner_backward, (split_factor, owner_tiles, owner_rows, owner_cols)).reshape(PERSONS, TRAITS)
        back = back.at[cols_all].add(weights * factor[rows_all])
        return diag_var[:, None] * solution_values + back

    solution_field = jnp.zeros((PERSONS, TRAITS), jnp.float32)
    residual = target
    direction = target
    norm_now = jnp.sum(residual * residual, axis=0)
    for step in range(ITERS):
        image = apply_operator(direction)
        alpha = norm_now / jnp.sum(direction * image, axis=0)
        solution_field = solution_field + alpha[None, :] * direction
        residual = residual - alpha[None, :] * image
        norm_next = jnp.sum(residual * residual, axis=0)
        direction = residual + (norm_next / norm_now)[None, :] * direction
        norm_now = norm_next
    return solution_field, residual
```

```python
import functools

import jax
import jax.numpy as jnp
from jax import lax
from jax.experimental import pallas as pl
from jax.experimental.pallas import tpu as pltpu
from jax.sharding import PartitionSpec as P

ITERS = 3


PRECISION_HIGH = lax.Precision.HIGHEST


def block_rank(owner, groups):
    marker_flags = (owner[:, None] == jnp.arange(groups, dtype=jnp.int32)[None, :]).astype(
        jnp.int32
    )
    ranks = jnp.cumsum(marker_flags, axis=0) - 1
    return jnp.sum(ranks * marker_flags, axis=1)


def forward_tile_map(solution_values, tiles, trow, tcol, nblocks):
    blocks = solution_values.reshape(nblocks, 64, solution_values.shape[1])
    selected_entries = blocks[tcol]
    operator_products = jnp.einsum(
        "olh,ohj->olj", tiles, selected_entries, precision=PRECISION_HIGH
    )
    marker_flags = (trow[None, :] == jnp.arange(nblocks, dtype=jnp.int32)[:, None]).astype(
        jnp.float32
    )
    return jnp.einsum(
        "fo,ouh->fuh", marker_flags, operator_products, precision=PRECISION_HIGH
    ).reshape(solution_values.shape)


def tile_backward(solution_values, tiles, trow, tcol, nblocks):
    blocks = solution_values.reshape(nblocks, 64, solution_values.shape[1])
    selected_entries = blocks[trow]
    operator_products = jnp.einsum(
        "zxp,zxm->zpm", tiles, selected_entries, precision=PRECISION_HIGH
    )
    marker_flags = (tcol[None, :] == jnp.arange(nblocks, dtype=jnp.int32)[:, None]).astype(
        jnp.float32
    )
    return jnp.einsum(
        "fo,ouh->fuh", marker_flags, operator_products, precision=PRECISION_HIGH
    ).reshape(solution_values.shape)


def total_squares(solution_values):
    return lax.psum(jnp.sum(solution_values * solution_values, axis=0), "fam")


def local(
    pheno,
    match,
    diag_var,
    tiles,
    tile_row_family,
    tile_cols,
    rel_row,
    rel_peer,
    rel_slot,
    rel_weight,
):
    groups = lax.axis_size("fam")
    persons = pheno.shape[0]
    nblocks = persons // 64
    tile_set = tiles.reshape(tiles.shape[0], 64, 64)
    peers = rel_peer[:, 0]
    weights = rel_weight[:, None]
    columns = pheno.shape[1]
    owner = match // persons
    slot = match % persons
    cap = 2 * persons // groups
    dest = owner * cap + block_rank(owner, groups)
    send_vals = jnp.zeros((groups * cap, columns), jnp.float32).at[dest].set(pheno)
    send_slots = jnp.full((groups * cap,), -1.0, jnp.float32).at[dest].set(slot.astype(jnp.float32))
    got_vals, got_slots = (
        lax.all_to_all(send_vals, "fam", split_axis=0, concat_axis=0, tiled=True),
        lax.all_to_all(send_slots, "fam", split_axis=0, concat_axis=0, tiled=True),
    )
    landing = jnp.where(got_slots >= 0, got_slots.astype(jnp.int32), persons)
    target = jnp.zeros((persons, columns), jnp.float32).at[landing].set(got_vals, mode="drop")
    entries = rel_row.shape[0]
    rcap = 2 * entries // groups
    rdest = peers * rcap + block_rank(peers, groups)
    asks = jnp.full((groups * rcap,), -1, jnp.int32).at[rdest].set(rel_slot)
    incoming = lax.all_to_all(asks, "fam", split_axis=0, concat_axis=0, tiled=True)
    valid = incoming >= 0
    picked_slot = jnp.where(valid, incoming, 0)
    arriving = jnp.where(valid, incoming, persons)
    solution_field = jnp.zeros((persons, columns), jnp.float32)
    residual = target
    direction = target
    norm_now = total_squares(residual)
    for step in range(ITERS):
        factor_part = forward_tile_map(direction, tile_set, tile_row_family, tile_cols, nblocks)
        outgoing = jnp.where(valid[:, None], direction[picked_slot], 0.0)
        answers = lax.all_to_all(outgoing, "fam", split_axis=0, concat_axis=0, tiled=True)
        factor_part = factor_part.at[rel_row].add(weights * answers[rdest])
        factor_part = lax.psum(factor_part, "rep")
        part = tile_backward(factor_part, tile_set, tile_row_family, tile_cols, nblocks)
        pushed = (
            jnp.zeros((groups * rcap, columns), jnp.float32)
            .at[rdest]
            .set(weights * factor_part[rel_row])
        )
        landed = lax.all_to_all(pushed, "fam", split_axis=0, concat_axis=0, tiled=True)
        part = part.at[arriving].add(landed, mode="drop")
        part = lax.psum(part, "rep")
        image = diag_var[:, None] * direction + part
        curvature = lax.psum(jnp.sum(direction * image, axis=0), "fam")
        alpha = norm_now / curvature
        solution_field = solution_field + alpha[None, :] * direction
        residual = residual - alpha[None, :] * image
        norm_next = total_squares(residual)
        direction = residual + (norm_next / norm_now)[None, :] * direction
        norm_now = norm_next
    return (solution_field, residual)


def split_terms(values):
    high = values.astype(jnp.bfloat16)
    low = (values - high.astype(jnp.float32)).astype(jnp.bfloat16)
    return jnp.concatenate([high, low], axis=1)


def fold(values):
    half = values.shape[1] // 2
    return values[:, :half] + values[:, half:]


def mm(left, right):
    return jnp.dot(left, right, preferred_element_type=jnp.float32)


def one_hot_rows(ref, index_col, rows, strip):
    width = ref.shape[1]

    def body(i, _):
        at = pl.ds(pl.multiple_of(i * strip, strip), strip)
        lane = lax.broadcasted_iota(jnp.int32, (strip, width), 1)
        ref[at, :] = jnp.where(index_col[at, :] == lane, 1.0, 0.0).astype(jnp.bfloat16)
        return 0

    lax.fori_loop(0, rows // strip, body, 0)


def one_hot_cols(ref, index_row, rows, strip):
    width = ref.shape[1]

    def body(i, _):
        at = pl.ds(pl.multiple_of(i * strip, strip), strip)
        sub = lax.broadcasted_iota(jnp.int32, (strip, width), 0) + i * strip
        ref[at, :] = jnp.where(index_row[...] == sub, 1.0, 0.0).astype(jnp.bfloat16)
        return 0

    lax.fori_loop(0, rows // strip, body, 0)


def build_factor(owners, per_owner, nblk, trow, tcol, tiles, kb, ktb, khi, klo, kthi, ktlo):
    def owner(o, _):
        kb[...] = jnp.zeros_like(kb)
        ktb[...] = jnp.zeros_like(ktb)

        def place(t, _):
            e = o * per_owner + t
            pair = tiles[e]
            tile = jnp.concatenate([pair[:, :64], pair[:, 64:]], axis=0)
            a, b = trow[e], tcol[e]
            kb[b, pl.ds(pl.multiple_of(a * 64, 64), 64), :] = tile
            ktb[a, pl.ds(pl.multiple_of(b * 64, 64), 64), :] = tile.T
            return 0

        lax.fori_loop(0, per_owner, place, 0)
        for src, hi, lo in ((kb, khi, klo), (ktb, kthi, ktlo)):
            full = jnp.concatenate([src[j] for j in range(nblk)], axis=1)
            high = full.astype(jnp.bfloat16)
            hi[o] = high
            lo[o] = (full - high.astype(jnp.float32)).astype(jnp.bfloat16)
        return 0

    lax.fori_loop(0, owners, owner, 0)


def group_kernel(
    owners,
    persons,
    per_owner,
    trow,
    tcol,
    me_ref,
    tiles,
    match_row,
    diag,
    col_row,
    col_col,
    row_row,
    row_col,
    weight,
    pheno,
    x_out,
    r_out,
    kb,
    ktb,
    khi,
    klo,
    kthi,
    ktlo,
    pm,
    c,
    ct,
    rsel,
    rselt,
    d,
    r,
    dcat,
    ycat,
    hcat,
):
    every = owners * persons
    entries = c.shape[0]
    eown = entries // owners
    n = pheno.shape[1]
    nblk = persons // 64
    me = me_ref[0]

    @pl.when(pl.program_id(0) == 0)
    def _():
        build_factor(
            owners, per_owner, nblk, trow, tcol, tiles, kb, ktb, khi, klo, kthi, ktlo
        )
        one_hot_cols(pm, match_row, every, 64)
        one_hot_rows(c, col_col, entries, 64)
        one_hot_cols(ct, col_row, every, 64)
        one_hot_rows(rsel, row_col, entries, 64)
        for o in range(owners):
            lane = row_row[:, o * eown : (o + 1) * eown]
            sub = lax.broadcasted_iota(jnp.int32, (persons, eown), 0)
            rselt[o] = jnp.where(lane == sub, 1.0, 0.0).astype(jnp.bfloat16)

    def person(o):
        return pl.ds(pl.multiple_of(o * persons, persons), persons)

    def entry(o):
        return pl.ds(pl.multiple_of(o * eown, eown), eown)

    zero = jnp.zeros((1, n), jnp.float32)

    def colsum(v):
        return jnp.sum(v, axis=0, keepdims=True)

    ycat[...] = split_terms(pheno[...])

    def begin(o, carry):
        rr, dd = carry
        t = fold(mm(pm[person(o), :], ycat[...]))
        r[person(o), :] = t
        d[person(o), :] = t
        dcat[person(o), :] = split_terms(t)
        square = t * t
        return rr + colsum(square), dd + colsum(square * diag[person(o), :])

    rr, dd = lax.fori_loop(0, owners, begin, (zero, zero))

    def forward(o, yy):
        g = fold(mm(c[entry(o), :], dcat[...])) * weight[entry(o), :]
        near = dcat[person(o), :]
        y = fold(mm(khi[o], near) + mm(rselt[o], split_terms(g)))
        y = y + mm(klo[o], near[:, :n])
        ys = split_terms(y)
        ycat[person(o), :] = ys
        h = fold(mm(rsel[entry(o), :], ys)) * weight[entry(o), :]
        hcat[entry(o), :] = split_terms(h)
        return yy + colsum(y * y)

    def image(o):
        ys = ycat[person(o), :]
        back = fold(mm(kthi[o], ys) + mm(ct[person(o), :], hcat[...]))
        back = back + mm(ktlo[o], ys[:, :n])
        return diag[person(o), :] * d[person(o), :] + back

    for step in range(ITERS):
        yy = lax.fori_loop(0, owners, forward, zero)
        alpha = rr / (yy + dd)
        move = alpha * d[person(me), :]
        if step == 0:
            x_out[...] = move
        else:
            x_out[...] = x_out[...] + move
        if step == ITERS - 1:
            r_out[...] = r[person(me), :] - alpha * image(me)
            break

        def descend(o, acc):
            left = r[person(o), :] - alpha * image(o)
            r[person(o), :] = left
            return acc + colsum(left * left)

        nxt = lax.fori_loop(0, owners, descend, zero)
        beta = nxt / rr
        rr = nxt

        def turn(o, acc):
            v = r[person(o), :] + beta * d[person(o), :]
            d[person(o), :] = v
            dcat[person(o), :] = split_terms(v)
            return acc + colsum(v * v * diag[person(o), :])

        dd = lax.fori_loop(0, owners, turn, zero)


def local_group(
    pheno,
    match,
    diag_var,
    tiles,
    tile_row_family,
    tile_cols,
    rel_row,
    rel_peer,
    rel_slot,
    rel_weight,
):
    owners = lax.axis_size("fam")
    reps = lax.axis_size("rep")
    traits = lax.axis_size("trait")
    persons, columns = pheno.shape
    mine = columns // reps
    n = 128
    me = lax.axis_index("fam")
    rep = lax.axis_index("rep")
    held = tiles.shape[0]
    share = held // traits
    pairs = tiles.reshape(held, 32, 128)
    pairs = lax.dynamic_slice_in_dim(pairs, lax.axis_index("trait") * share, share, 0)
    pairs = lax.all_gather(pairs, ("fam", "rep", "trait"), tiled=True)
    col = rel_peer[:, 0] * persons + rel_slot
    inner = rel_row % 64
    row = rel_row - inner + (inner % 2) * 32 + inner // 2
    ints = (match, tile_row_family, tile_cols, col, row)
    packed = jnp.concatenate([v.astype(jnp.float32) for v in ints] + [diag_var, rel_weight])
    everyone = lax.all_gather(packed, ("fam", "rep")).reshape(owners, reps, -1)
    sizes = [v.shape[0] for v in ints] + [persons, rel_row.shape[0]]
    parts, at = [], 0
    for size in sizes:
        parts.append(everyone[:, :, at : at + size])
        at += size
    match_all = parts[0][:, 0].reshape(1, -1).astype(jnp.int32)
    trow = parts[1].reshape(-1).astype(jnp.int32)
    tcol = parts[2].reshape(-1).astype(jnp.int32)
    col_all = parts[3].reshape(-1).astype(jnp.int32)
    row_all = parts[4].reshape(-1).astype(jnp.int32)
    diag_all = parts[5][:, 0].reshape(-1, 1)
    weight_all = parts[6].reshape(-1, 1)
    part = lax.dynamic_slice_in_dim(pheno, rep * mine, mine, 1)
    gathered = lax.all_gather(part, "fam", tiled=True)
    every = owners * persons
    entries = col_all.shape[0]
    eown = entries // owners
    nblk = persons // 64
    smem = pl.BlockSpec(memory_space=pltpu.SMEM)
    vmem = pl.BlockSpec(memory_space=pltpu.VMEM)
    bf = jnp.bfloat16
    x, r = pl.pallas_call(
        functools.partial(group_kernel, owners, persons, held * reps),
        grid=(mine // n,),
        out_shape=[jax.ShapeDtypeStruct((persons, mine), jnp.float32)] * 2,
        in_specs=[smem] * 3 + [vmem] * 8 + [pl.BlockSpec((every, n), lambda i: (0, i))],
        out_specs=[pl.BlockSpec((persons, n), lambda i: (0, i))] * 2,
        scratch_shapes=[
            pltpu.VMEM((nblk, persons, 64), jnp.float32),
            pltpu.VMEM((nblk, persons, 64), jnp.float32),
            pltpu.VMEM((owners, persons, persons), bf),
            pltpu.VMEM((owners, persons, persons), bf),
            pltpu.VMEM((owners, persons, persons), bf),
            pltpu.VMEM((owners, persons, persons), bf),
            pltpu.VMEM((every, every), bf),
            pltpu.VMEM((entries, every), bf),
            pltpu.VMEM((every, entries), bf),
            pltpu.VMEM((entries, persons), bf),
            pltpu.VMEM((owners, persons, eown), bf),
            pltpu.VMEM((every, n), jnp.float32),
            pltpu.VMEM((every, n), jnp.float32),
            pltpu.VMEM((every, 2 * n), bf),
            pltpu.VMEM((every, 2 * n), bf),
            pltpu.VMEM((entries, 2 * n), bf),
        ],
        compiler_params=pltpu.CompilerParams(vmem_limit_bytes=60 * 2**20),
    )(
        trow,
        tcol,
        me.reshape(1),
        pairs,
        match_all,
        diag_all,
        col_all.reshape(1, -1),
        col_all.reshape(-1, 1),
        row_all.reshape(1, -1),
        row_all.reshape(-1, 1),
        weight_all,
        gathered,
    )
    x = lax.all_gather(x, "rep", axis=1, tiled=True)
    r = lax.all_gather(r, "rep", axis=1, tiled=True)
    return x, r


def solution(mesh):
    placed = (
        P(("groups", "fam"), "trait"),
        P(("groups", "fam")),
        P(("groups", "fam")),
        P(("groups", "fam", "rep"), None),
        P(("groups", "fam", "rep")),
        P(("groups", "fam", "rep")),
        P(("groups", "fam", "rep")),
        P(("groups", "fam", "rep"), None),
        P(("groups", "fam", "rep")),
        P(("groups", "fam", "rep")),
    )
    whole = mesh.shape["fam"] <= 4
    return jax.shard_map(
        local_group if whole else local,
        mesh=mesh,
        in_specs=placed,
        out_specs=(P(("groups", "fam"), "trait"), P(("groups", "fam"), "trait")),
        check_vma=False,
    )
```

```python
import functools

import jax
import jax.numpy as jnp
from jax import lax
from jax.experimental import pallas as pl
from jax.experimental.pallas import tpu as pltpu
from jax.sharding import PartitionSpec as P

ITERS = 3


PRECISION_HIGH = lax.Precision.HIGHEST


def block_rank(owner, groups):
    marker_flags = (owner[:, None] == jnp.arange(groups, dtype=jnp.int32)[None, :]).astype(
        jnp.int32
    )
    ranks = jnp.cumsum(marker_flags, axis=0) - 1
    return jnp.sum(ranks * marker_flags, axis=1)


def forward_tile_map(solution_values, tiles, trow, tcol, nblocks):
    blocks = solution_values.reshape(nblocks, 64, solution_values.shape[1])
    selected_entries = blocks[tcol]
    operator_products = jnp.einsum(
        "olh,ohj->olj", tiles, selected_entries, precision=PRECISION_HIGH
    )
    marker_flags = (trow[None, :] == jnp.arange(nblocks, dtype=jnp.int32)[:, None]).astype(
        jnp.float32
    )
    return jnp.einsum(
        "fo,ouh->fuh", marker_flags, operator_products, precision=PRECISION_HIGH
    ).reshape(solution_values.shape)


def tile_backward(solution_values, tiles, trow, tcol, nblocks):
    blocks = solution_values.reshape(nblocks, 64, solution_values.shape[1])
    selected_entries = blocks[trow]
    operator_products = jnp.einsum(
        "zxp,zxm->zpm", tiles, selected_entries, precision=PRECISION_HIGH
    )
    marker_flags = (tcol[None, :] == jnp.arange(nblocks, dtype=jnp.int32)[:, None]).astype(
        jnp.float32
    )
    return jnp.einsum(
        "fo,ouh->fuh", marker_flags, operator_products, precision=PRECISION_HIGH
    ).reshape(solution_values.shape)


def total_squares(solution_values):
    return lax.psum(jnp.sum(solution_values * solution_values, axis=0), "fam")


def local(
    pheno,
    match,
    diag_var,
    tiles,
    tile_row_family,
    tile_cols,
    rel_row,
    rel_peer,
    rel_slot,
    rel_weight,
):
    groups = lax.axis_size("fam")
    persons = pheno.shape[0]
    nblocks = persons // 64
    tile_set = tiles.reshape(tiles.shape[0], 64, 64)
    peers = rel_peer[:, 0]
    weights = rel_weight[:, None]
    columns = pheno.shape[1]
    owner = match // persons
    slot = match % persons
    cap = 2 * persons // groups
    dest = owner * cap + block_rank(owner, groups)
    send_vals = jnp.zeros((groups * cap, columns), jnp.float32).at[dest].set(pheno)
    send_slots = jnp.full((groups * cap,), -1.0, jnp.float32).at[dest].set(slot.astype(jnp.float32))
    got_vals, got_slots = (
        lax.all_to_all(send_vals, "fam", split_axis=0, concat_axis=0, tiled=True),
        lax.all_to_all(send_slots, "fam", split_axis=0, concat_axis=0, tiled=True),
    )
    landing = jnp.where(got_slots >= 0, got_slots.astype(jnp.int32), persons)
    target = jnp.zeros((persons, columns), jnp.float32).at[landing].set(got_vals, mode="drop")
    entries = rel_row.shape[0]
    rcap = 2 * entries // groups
    rdest = peers * rcap + block_rank(peers, groups)
    asks = jnp.full((groups * rcap,), -1, jnp.int32).at[rdest].set(rel_slot)
    incoming = lax.all_to_all(asks, "fam", split_axis=0, concat_axis=0, tiled=True)
    valid = incoming >= 0
    picked_slot = jnp.where(valid, incoming, 0)
    arriving = jnp.where(valid, incoming, persons)
    solution_field = jnp.zeros((persons, columns), jnp.float32)
    residual = target
    direction = target
    norm_now = total_squares(residual)
    for step in range(ITERS):
        factor_part = forward_tile_map(direction, tile_set, tile_row_family, tile_cols, nblocks)
        outgoing = jnp.where(valid[:, None], direction[picked_slot], 0.0)
        answers = lax.all_to_all(outgoing, "fam", split_axis=0, concat_axis=0, tiled=True)
        factor_part = factor_part.at[rel_row].add(weights * answers[rdest])
        factor_part = lax.psum(factor_part, "rep")
        part = tile_backward(factor_part, tile_set, tile_row_family, tile_cols, nblocks)
        pushed = (
            jnp.zeros((groups * rcap, columns), jnp.float32)
            .at[rdest]
            .set(weights * factor_part[rel_row])
        )
        landed = lax.all_to_all(pushed, "fam", split_axis=0, concat_axis=0, tiled=True)
        part = part.at[arriving].add(landed, mode="drop")
        part = lax.psum(part, "rep")
        image = diag_var[:, None] * direction + part
        curvature = lax.psum(jnp.sum(direction * image, axis=0), "fam")
        alpha = norm_now / curvature
        solution_field = solution_field + alpha[None, :] * direction
        residual = residual - alpha[None, :] * image
        norm_next = total_squares(residual)
        direction = residual + (norm_next / norm_now)[None, :] * direction
        norm_now = norm_next
    return (solution_field, residual)


def split_terms(values):
    high = values.astype(jnp.bfloat16)
    low = (values - high.astype(jnp.float32)).astype(jnp.bfloat16)
    return jnp.concatenate([high, low], axis=1)


def fold(values):
    half = values.shape[1] // 2
    return values[:, :half] + values[:, half:]


def mm(left, right):
    return jnp.dot(left, right, preferred_element_type=jnp.float32)


def one_hot_rows(ref, index_col, rows, strip):
    width = ref.shape[1]

    def body(i, _):
        at = pl.ds(pl.multiple_of(i * strip, strip), strip)
        lane = lax.broadcasted_iota(jnp.int32, (strip, width), 1)
        ref[at, :] = jnp.where(index_col[at, :] == lane, 1.0, 0.0).astype(jnp.bfloat16)
        return 0

    lax.fori_loop(0, rows // strip, body, 0)


def one_hot_cols(ref, index_row, rows, strip):
    width = ref.shape[1]

    def body(i, _):
        at = pl.ds(pl.multiple_of(i * strip, strip), strip)
        sub = lax.broadcasted_iota(jnp.int32, (strip, width), 0) + i * strip
        ref[at, :] = jnp.where(index_row[...] == sub, 1.0, 0.0).astype(jnp.bfloat16)
        return 0

    lax.fori_loop(0, rows // strip, body, 0)


def copy_to(src, dst, sems, at, **where):
    send, recv = sems
    return pltpu.make_async_remote_copy(
        src_ref=src,
        dst_ref=dst,
        send_sem=send.at[at],
        recv_sem=recv.at[at],
        device_id=where,
        device_id_type=pl.DeviceIdType.MESH,
    )


def group_kernel(
    owners,
    imeta,
    fmeta,
    pairs,
    pheno,
    x_out,
    r_out,
    imeta_all,
    fmeta_all,
    tiles_all,
    ph_all,
    inv_v,
    inv,
    match_row,
    col_row,
    row_row,
    col_col,
    row_col,
    weight,
    diag,
    khi,
    klo,
    kthi,
    ktlo,
    pm,
    c,
    ct,
    rsel,
    rselt,
    d,
    r,
    xs,
    dcat,
    ycat,
    hcat,
    meta_send,
    meta_recv,
    tile_send,
    tile_recv,
    ph_send,
    ph_recv,
    out_send,
    out_recv,
    local_sem,
):
    persons = pheno.shape[0]
    every = owners * persons
    entries = c.shape[0]
    eown = entries // owners
    n = d.shape[1]
    held = pairs.shape[0]
    share = held // 2
    half = persons // 2
    nblk = persons // 64
    lists = 2 * owners
    blank = lists * held
    f = lax.axis_index("fam")
    t = lax.axis_index("trait")
    rep = lax.axis_index("rep")
    other = 1 - rep
    across = 1 - t
    me = f * 2 + rep
    peers = [lax.rem(f + k, owners) for k in range(1, owners)]
    sources = [lax.rem(f + owners - k, owners) for k in range(1, owners)]

    barrier = pltpu.get_barrier_semaphore()
    greet = [dict(fam=p, rep=q) for p in peers for q in (rep, other)]
    greet += [dict(rep=other), dict(trait=across)]
    for g in greet:
        pl.semaphore_signal(barrier, inc=1, device_id=g, device_id_type=pl.DeviceIdType.MESH)
    pl.semaphore_wait(barrier, len(greet))

    meta_sems = (meta_send, meta_recv)
    meta_copies = []
    at = 0
    for own, all_ in ((imeta, imeta_all), (fmeta, fmeta_all)):
        for g in greet[:-1]:
            cp = copy_to(own, all_.at[me], meta_sems, at, **g)
            cp.start()
            meta_copies.append(cp)
            at += 1

    def tiles_of(source, who, part):
        first = (source * 2 + who) * held + part * share
        return tiles_all.at[pl.ds(first, share)]

    tile_sems = (tile_send, tile_recv)
    k3 = owners - 1
    along = []
    for k, p in enumerate(peers):
        cp = copy_to(pairs.at[pl.ds(t * share, share)], tiles_of(f, rep, t), tile_sems, k, fam=p)
        cp.start()
        along.append(cp)
    own_tiles = tiles_all.at[pl.ds(me * held, held)]
    tile_home = copy_to(pairs, own_tiles, tile_sems, 4 * k3, rep=other)
    tile_home.start()

    ph_sems = (ph_send, ph_recv)
    ph_along = []
    for k, p in enumerate(peers):
        cp = copy_to(
            pheno.at[pl.ds(rep * half, half), pl.ds(pl.multiple_of(p * n, n), n)],
            ph_all.at[pl.ds(f * persons + rep * half, half)],
            ph_sems,
            k,
            fam=p,
        )
        cp.start()
        ph_along.append(cp)

    keep = [
        pltpu.make_async_copy(imeta, imeta_all.at[me], local_sem.at[0]),
        pltpu.make_async_copy(fmeta, fmeta_all.at[me], local_sem.at[1]),
        pltpu.make_async_copy(pairs, own_tiles, local_sem.at[2]),
        pltpu.make_async_copy(
            pheno.at[:, pl.ds(pl.multiple_of(f * n, n), n)],
            ph_all.at[pl.ds(f * persons, persons)],
            local_sem.at[3],
        ),
    ]
    for cp in keep:
        cp.start()
    tiles_all[blank] = jnp.zeros(tiles_all.shape[1:], jnp.float32)
    for cp in keep:
        cp.wait()
    for cp in meta_copies:
        cp.wait()

    inv_v[...] = jnp.zeros(inv_v.shape, jnp.int32)
    pos_lane = lax.broadcasted_iota(jnp.int32, (held, n), 1)
    tile_id = lax.broadcasted_iota(jnp.int32, (held, n), 0)
    for o in range(owners):
        found = jnp.zeros((1, n), jnp.int32)
        for q in range(2):
            j = 2 * o + q
            im = imeta_all[j]
            imt = im.T
            at = slice(j * n, (j + 1) * n)
            col_row[:, at] = im[4:5]
            row_row[:, at] = im[5:6]
            col_col[at, :] = imt[:, 4:5]
            row_col[at, :] = imt[:, 5:6]
            fmt = fmeta_all[j].T
            weight[at, :] = fmt[:, 4:5]
            hit = jnp.where(imt[:held, 6:7] == pos_lane, tile_id + (j * held + 1), 0)
            found = jnp.maximum(found, jnp.max(hit, axis=0, keepdims=True))
            if q == 0:
                for i in range(persons // n):
                    at = slice(o * persons + i * n, o * persons + (i + 1) * n)
                    match_row[:, at] = im[i : i + 1]
                    diag[at, :] = fmt[:, i : i + 1]
        inv_v[o : o + 1, :] = jnp.where(found == 0, blank, found - 1)
    to_scalar = pltpu.make_async_copy(inv_v, inv, local_sem.at[4])
    to_scalar.start()

    one_hot_rows(c, col_col, entries, 64)
    one_hot_cols(ct, col_row, every, 64)
    tile_across, tile_side = [], []
    for k, s in enumerate(sources):
        along[k].wait()
        cp = copy_to(tiles_of(s, rep, t), tiles_of(s, rep, t), tile_sems, k3 + k, trait=across)
        cp.start()
        tile_across.append(cp)
        cp = copy_to(tiles_of(s, rep, t), tiles_of(s, rep, t), tile_sems, 2 * k3 + k, rep=other)
        cp.start()
        tile_side.append(cp)
    one_hot_rows(rsel, row_col, entries, 64)
    for o in range(owners):
        lane = row_row[:, o * eown : (o + 1) * eown]
        sub = lax.broadcasted_iota(jnp.int32, (persons, eown), 0)
        rselt[o] = jnp.where(lane == sub, 1.0, 0.0).astype(jnp.bfloat16)
    for k, s in enumerate(sources):
        tile_across[k].wait()
        part = tiles_of(s, rep, across)
        cp = copy_to(part, part, tile_sems, 3 * k3 + k, rep=other)
        cp.start()
        tile_side.append(cp)
    one_hot_cols(pm, match_row, every, 64)
    ph_side = []
    for k, s in enumerate(sources):
        ph_along[k].wait()
        part = ph_all.at[pl.ds(s * persons + rep * half, half)]
        cp = copy_to(part, part, ph_sems, k3 + k, rep=other)
        cp.start()
        ph_side.append(cp)
    to_scalar.wait()
    tile_home.wait()
    for cp in tile_side:
        cp.wait()

    def factor(o, _):
        for a2 in range(nblk // 2):
            rows = []
            for a in (2 * a2, 2 * a2 + 1):
                got = [tiles_all[inv[o, a * nblk + b]] for b in range(nblk)]
                rows.append(jnp.concatenate([g[:, :64] for g in got], axis=1))
                rows.append(jnp.concatenate([g[:, 64:] for g in got], axis=1))
            full = jnp.concatenate(rows, axis=0)
            at = slice(a2 * 128, (a2 + 1) * 128)
            high = full.astype(jnp.bfloat16)
            khi[o, at, :] = high
            klo[o, at, :] = (full - high.astype(jnp.float32)).astype(jnp.bfloat16)
            full = full.T
            high = full.astype(jnp.bfloat16)
            kthi[o, :, at] = high
            ktlo[o, :, at] = (full - high.astype(jnp.float32)).astype(jnp.bfloat16)
        return 0

    lax.fori_loop(0, owners, factor, 0)

    def person(o):
        return pl.ds(pl.multiple_of(o * persons, persons), persons)

    def entry(o):
        return pl.ds(pl.multiple_of(o * eown, eown), eown)

    zero = jnp.zeros((1, n), jnp.float32)

    def colsum(v):
        return jnp.sum(v, axis=0, keepdims=True)

    for cp in ph_side:
        cp.wait()
    ycat[...] = split_terms(ph_all[...])

    def begin(o, carry):
        rr, dd = carry
        v = fold(mm(pm[person(o), :], ycat[...]))
        r[person(o), :] = v
        d[person(o), :] = v
        dcat[person(o), :] = split_terms(v)
        square = v * v
        return rr + colsum(square), dd + colsum(square * diag[person(o), :])

    rr, dd = lax.fori_loop(0, owners, begin, (zero, zero))

    def forward(o, yy):
        g = fold(mm(c[entry(o), :], dcat[...])) * weight[entry(o), :]
        near = dcat[person(o), :]
        y = fold(mm(khi[o], near) + mm(rselt[o], split_terms(g)))
        y = y + mm(klo[o], near[:, :n])
        ys = split_terms(y)
        ycat[person(o), :] = ys
        h = fold(mm(rsel[entry(o), :], ys)) * weight[entry(o), :]
        hcat[entry(o), :] = split_terms(h)
        return yy + colsum(y * y)

    def image(o):
        ys = ycat[person(o), :]
        back = fold(mm(kthi[o], ys) + mm(ct[person(o), :], hcat[...]))
        back = back + mm(ktlo[o], ys[:, :n])
        return diag[person(o), :] * d[person(o), :] + back

    def advance(alpha, first):
        def body(o, _):
            move = alpha * d[person(o), :]
            xs[person(o), :] = move if first else xs[person(o), :] + move
            return 0

        lax.fori_loop(0, owners, body, 0)

    for step in range(ITERS - 1):
        yy = lax.fori_loop(0, owners, forward, zero)
        alpha = rr / (yy + dd)
        advance(alpha, step == 0)

        def descend(o, acc):
            left = r[person(o), :] - alpha * image(o)
            r[person(o), :] = left
            return acc + colsum(left * left)

        nxt = lax.fori_loop(0, owners, descend, zero)
        beta = nxt / rr
        rr = nxt

        def turn(o, acc):
            v = r[person(o), :] + beta * d[person(o), :]
            d[person(o), :] = v
            dcat[person(o), :] = split_terms(v)
            return acc + colsum(v * v * diag[person(o), :])

        dd = lax.fori_loop(0, owners, turn, zero)

    yy = lax.fori_loop(0, owners, forward, zero)
    alpha = rr / (yy + dd)
    advance(alpha, False)

    out_sems = (out_send, out_recv)
    mycols = pl.ds(pl.multiple_of(f * n, n), n)

    def give(src, dst, k, at):
        cp = copy_to(
            src.at[pl.ds(peers[k] * persons + rep * half, half)],
            dst.at[pl.ds(rep * half, half), mycols],
            out_sems,
            at,
            fam=peers[k],
        )
        cp.start()
        return cp

    out_along = [give(xs, x_out, k, k) for k in range(k3)]
    stay = [pltpu.make_async_copy(xs.at[pl.ds(f * persons, persons)], x_out.at[:, mycols], local_sem.at[5])]
    stay[0].start()
    for k in range(owners):
        o = peers[k] if k < k3 else f
        r[person(o), :] = r[person(o), :] - alpha * image(o)
        if k < k3:
            out_along.append(give(r, r_out, k, k3 + k))
    stay.append(
        pltpu.make_async_copy(r.at[pl.ds(f * persons, persons)], r_out.at[:, mycols], local_sem.at[6])
    )
    stay[1].start()
    out_side = []
    for i, cp in enumerate(out_along):
        cp.wait()
        dst = x_out if i < k3 else r_out
        s = sources[i % k3]
        part = dst.at[pl.ds(rep * half, half), pl.ds(pl.multiple_of(s * n, n), n)]
        side = copy_to(part, part, out_sems, 2 * k3 + i, rep=other)
        side.start()
        out_side.append(side)
    for cp in out_side + stay:
        cp.wait()


def local_group(
    pheno,
    match,
    diag_var,
    tiles,
    tile_row_family,
    tile_cols,
    rel_row,
    rel_peer,
    rel_slot,
    rel_weight,
):
    owners = lax.axis_size("fam")
    persons, columns = pheno.shape
    n = columns // owners
    held = tiles.shape[0]
    nblk = persons // 64
    pairs = tiles.reshape(held, 32, 128)
    inner = rel_row % 64
    row = rel_row - inner + (inner % 2) * 32 + inner // 2
    col = rel_peer[:, 0] * persons + rel_slot
    place = jnp.pad(tile_row_family * nblk + tile_cols, (0, n - held), constant_values=-1)
    imeta = jnp.concatenate([match, col, row, place, place]).reshape(8, n)
    fmeta = jnp.concatenate([diag_var, rel_weight, rel_weight, rel_weight, rel_weight]).reshape(8, n)
    lists = 2 * owners
    every = owners * persons
    entries = lists * rel_row.shape[0]
    eown = entries // owners
    vmem = pl.BlockSpec(memory_space=pltpu.VMEM)
    bf, f32, i32 = jnp.bfloat16, jnp.float32, jnp.int32
    k3 = owners - 1
    dma = pltpu.SemaphoreType.DMA
    return pl.pallas_call(
        functools.partial(group_kernel, owners),
        out_shape=[jax.ShapeDtypeStruct((persons, columns), f32)] * 2,
        in_specs=[vmem] * 4,
        out_specs=[vmem] * 2,
        scratch_shapes=[
            pltpu.VMEM((lists, 8, n), i32),
            pltpu.VMEM((lists, 8, n), f32),
            pltpu.VMEM((lists * held + 1, 32, 128), f32),
            pltpu.VMEM((every, n), f32),
            pltpu.VMEM((8, n), i32),
            pltpu.SMEM((8, n), i32),
            pltpu.VMEM((1, every), i32),
            pltpu.VMEM((1, entries), i32),
            pltpu.VMEM((1, entries), i32),
            pltpu.VMEM((entries, 1), i32),
            pltpu.VMEM((entries, 1), i32),
            pltpu.VMEM((entries, 1), f32),
            pltpu.VMEM((every, 1), f32),
            pltpu.VMEM((owners, persons, persons), bf),
            pltpu.VMEM((owners, persons, persons), bf),
            pltpu.VMEM((owners, persons, persons), bf),
            pltpu.VMEM((owners, persons, persons), bf),
            pltpu.VMEM((every, every), bf),
            pltpu.VMEM((entries, every), bf),
            pltpu.VMEM((every, entries), bf),
            pltpu.VMEM((entries, persons), bf),
            pltpu.VMEM((owners, persons, eown), bf),
            pltpu.VMEM((every, n), f32),
            pltpu.VMEM((every, n), f32),
            pltpu.VMEM((every, n), f32),
            pltpu.VMEM((every, 2 * n), bf),
            pltpu.VMEM((every, 2 * n), bf),
            pltpu.VMEM((entries, 2 * n), bf),
            dma((2 * lists - 2,)),
            dma((2 * lists - 2,)),
            dma((4 * k3 + 1,)),
            dma((4 * k3 + 1,)),
            dma((2 * k3,)),
            dma((2 * k3,)),
            dma((4 * k3,)),
            dma((4 * k3,)),
            dma((7,)),
        ],
        compiler_params=pltpu.CompilerParams(
            vmem_limit_bytes=60 * 2**20, collective_id=0, has_side_effects=True
        ),
    )(imeta, fmeta, pairs, pheno)


def solution(mesh):
    placed = (
        P(("groups", "fam"), "trait"),
        P(("groups", "fam")),
        P(("groups", "fam")),
        P(("groups", "fam", "rep"), None),
        P(("groups", "fam", "rep")),
        P(("groups", "fam", "rep")),
        P(("groups", "fam", "rep")),
        P(("groups", "fam", "rep"), None),
        P(("groups", "fam", "rep")),
        P(("groups", "fam", "rep")),
    )
    whole = mesh.shape["fam"] == 4 and mesh.shape["trait"] == 2 and mesh.shape["rep"] == 2
    return jax.shard_map(
        local_group if whole else local,
        mesh=mesh,
        in_specs=placed,
        out_specs=(P(("groups", "fam"), "trait"), P(("groups", "fam"), "trait")),
        check_vma=False,
    )
```

```python
import functools

import jax
import jax.numpy as jnp
from jax import lax
from jax.experimental import pallas as pl
from jax.experimental.pallas import tpu as pltpu
from jax.sharding import PartitionSpec as P

ITERS = 3


PRECISION_HIGH = lax.Precision.HIGHEST


def block_rank(owner, groups):
    marker_flags = (owner[:, None] == jnp.arange(groups, dtype=jnp.int32)[None, :]).astype(
        jnp.int32
    )
    ranks = jnp.cumsum(marker_flags, axis=0) - 1
    return jnp.sum(ranks * marker_flags, axis=1)


def forward_tile_map(solution_values, tiles, trow, tcol, nblocks):
    blocks = solution_values.reshape(nblocks, 64, solution_values.shape[1])
    selected_entries = blocks[tcol]
    operator_products = jnp.einsum(
        "olh,ohj->olj", tiles, selected_entries, precision=PRECISION_HIGH
    )
    marker_flags = (trow[None, :] == jnp.arange(nblocks, dtype=jnp.int32)[:, None]).astype(
        jnp.float32
    )
    return jnp.einsum(
        "fo,ouh->fuh", marker_flags, operator_products, precision=PRECISION_HIGH
    ).reshape(solution_values.shape)


def tile_backward(solution_values, tiles, trow, tcol, nblocks):
    blocks = solution_values.reshape(nblocks, 64, solution_values.shape[1])
    selected_entries = blocks[trow]
    operator_products = jnp.einsum(
        "zxp,zxm->zpm", tiles, selected_entries, precision=PRECISION_HIGH
    )
    marker_flags = (tcol[None, :] == jnp.arange(nblocks, dtype=jnp.int32)[:, None]).astype(
        jnp.float32
    )
    return jnp.einsum(
        "fo,ouh->fuh", marker_flags, operator_products, precision=PRECISION_HIGH
    ).reshape(solution_values.shape)


def total_squares(solution_values):
    return lax.psum(jnp.sum(solution_values * solution_values, axis=0), "fam")


def local(
    pheno,
    match,
    diag_var,
    tiles,
    tile_row_family,
    tile_cols,
    rel_row,
    rel_peer,
    rel_slot,
    rel_weight,
):
    groups = lax.axis_size("fam")
    persons = pheno.shape[0]
    nblocks = persons // 64
    tile_set = tiles.reshape(tiles.shape[0], 64, 64)
    peers = rel_peer[:, 0]
    weights = rel_weight[:, None]
    columns = pheno.shape[1]
    owner = match // persons
    slot = match % persons
    cap = 2 * persons // groups
    dest = owner * cap + block_rank(owner, groups)
    send_vals = jnp.zeros((groups * cap, columns), jnp.float32).at[dest].set(pheno)
    send_slots = jnp.full((groups * cap,), -1.0, jnp.float32).at[dest].set(slot.astype(jnp.float32))
    got_vals, got_slots = (
        lax.all_to_all(send_vals, "fam", split_axis=0, concat_axis=0, tiled=True),
        lax.all_to_all(send_slots, "fam", split_axis=0, concat_axis=0, tiled=True),
    )
    landing = jnp.where(got_slots >= 0, got_slots.astype(jnp.int32), persons)
    target = jnp.zeros((persons, columns), jnp.float32).at[landing].set(got_vals, mode="drop")
    entries = rel_row.shape[0]
    rcap = 2 * entries // groups
    rdest = peers * rcap + block_rank(peers, groups)
    asks = jnp.full((groups * rcap,), -1, jnp.int32).at[rdest].set(rel_slot)
    incoming = lax.all_to_all(asks, "fam", split_axis=0, concat_axis=0, tiled=True)
    valid = incoming >= 0
    picked_slot = jnp.where(valid, incoming, 0)
    arriving = jnp.where(valid, incoming, persons)
    solution_field = jnp.zeros((persons, columns), jnp.float32)
    residual = target
    direction = target
    norm_now = total_squares(residual)
    for step in range(ITERS):
        factor_part = forward_tile_map(direction, tile_set, tile_row_family, tile_cols, nblocks)
        outgoing = jnp.where(valid[:, None], direction[picked_slot], 0.0)
        answers = lax.all_to_all(outgoing, "fam", split_axis=0, concat_axis=0, tiled=True)
        factor_part = factor_part.at[rel_row].add(weights * answers[rdest])
        factor_part = lax.psum(factor_part, "rep")
        part = tile_backward(factor_part, tile_set, tile_row_family, tile_cols, nblocks)
        pushed = (
            jnp.zeros((groups * rcap, columns), jnp.float32)
            .at[rdest]
            .set(weights * factor_part[rel_row])
        )
        landed = lax.all_to_all(pushed, "fam", split_axis=0, concat_axis=0, tiled=True)
        part = part.at[arriving].add(landed, mode="drop")
        part = lax.psum(part, "rep")
        image = diag_var[:, None] * direction + part
        curvature = lax.psum(jnp.sum(direction * image, axis=0), "fam")
        alpha = norm_now / curvature
        solution_field = solution_field + alpha[None, :] * direction
        residual = residual - alpha[None, :] * image
        norm_next = total_squares(residual)
        direction = residual + (norm_next / norm_now)[None, :] * direction
        norm_now = norm_next
    return (solution_field, residual)


def split_terms(values):
    high = values.astype(jnp.bfloat16)
    low = (values - high.astype(jnp.float32)).astype(jnp.bfloat16)
    return jnp.concatenate([high, low], axis=1)


def fold(values):
    half = values.shape[1] // 2
    return values[:, :half] + values[:, half:]


def mm(left, right):
    return jnp.dot(left, right, preferred_element_type=jnp.float32)


def one_hot_rows(ref, index_col, rows, strip):
    width = ref.shape[1]

    def body(i, _):
        at = pl.ds(pl.multiple_of(i * strip, strip), strip)
        lane = lax.broadcasted_iota(jnp.int32, (strip, width), 1)
        ref[at, :] = jnp.where(index_col[at, :] == lane, 1.0, 0.0).astype(jnp.bfloat16)
        return 0

    lax.fori_loop(0, rows // strip, body, 0)


def one_hot_cols(ref, index_row, rows, strip):
    width = ref.shape[1]

    def body(i, _):
        at = pl.ds(pl.multiple_of(i * strip, strip), strip)
        sub = lax.broadcasted_iota(jnp.int32, (strip, width), 0) + i * strip
        ref[at, :] = jnp.where(index_row[...] == sub, 1.0, 0.0).astype(jnp.bfloat16)
        return 0

    lax.fori_loop(0, rows // strip, body, 0)


def copy_to(src, dst, sems, at, **where):
    send, recv = sems
    return pltpu.make_async_remote_copy(
        src_ref=src,
        dst_ref=dst,
        send_sem=send.at[at],
        recv_sem=recv.at[at],
        device_id=where,
        device_id_type=pl.DeviceIdType.MESH,
    )


def group_kernel(
    owners,
    match,
    diag_own,
    tiles,
    trow,
    tcol,
    rel_row,
    rel_peer,
    rel_slot,
    rel_weight,
    pheno,
    x_out,
    r_out,
    imeta,
    fmeta,
    pairs,
    imeta_all,
    fmeta_all,
    tiles_all,
    ph_all,
    inv_v,
    inv,
    match_row,
    col_row,
    row_row,
    col_col,
    row_col,
    weight,
    diag,
    khi,
    klo,
    kthi,
    ktlo,
    pm,
    c,
    ct,
    rsel,
    rselt,
    d,
    r,
    got,
    al,
    al_all,
    dcat,
    ycat,
    hcat,
    meta_send,
    meta_recv,
    tile_send,
    tile_recv,
    ph_send,
    ph_recv,
    out_send,
    out_recv,
    relay_send,
    local_sem,
):
    persons = pheno.shape[0]
    every = owners * persons
    entries = c.shape[0]
    eown = entries // owners
    n = r.shape[1]
    held = pairs.shape[0]
    share = held // 2
    half = persons // 2
    nblk = persons // 64
    lists = 2 * owners
    blank = lists * held
    f = lax.axis_index("fam")
    t = lax.axis_index("trait")
    rep = lax.axis_index("rep")
    other = 1 - rep
    across = 1 - t
    me = f * 2 + rep
    peers = [lax.rem(f + k, owners) for k in range(1, owners)]
    sources = [lax.rem(f + owners - k, owners) for k in range(1, owners)]

    barrier = pltpu.get_barrier_semaphore()
    greet = [dict(fam=p, rep=q) for p in peers for q in (rep, other)]
    greet += [dict(rep=other), dict(trait=across)]
    for g in greet:
        pl.semaphore_signal(barrier, inc=1, device_id=g, device_id_type=pl.DeviceIdType.MESH)

    inner = rel_row[...] % 64
    imeta[...] = jnp.full(imeta.shape, -1, jnp.int32)
    fmeta[...] = jnp.zeros(fmeta.shape, jnp.float32)
    imeta[0 : persons // n, :] = match[...]
    imeta[4:5, :] = rel_peer[...] * persons + rel_slot[...]
    imeta[5:6, :] = rel_row[...] - inner + (inner % 2) * 32 + inner // 2
    imeta[6:7, 0:held] = trow[...] * nblk + tcol[...]
    fmeta[0 : persons // n, :] = diag_own[...]
    fmeta[4:5, :] = rel_weight[...]
    for i in range(32):
        pairs[:, i, :] = tiles[:, i * 128 : (i + 1) * 128]
    pl.semaphore_wait(barrier, len(greet))

    meta_sems = (meta_send, meta_recv)
    meta_copies = []
    at = 0
    for own, all_ in ((imeta, imeta_all), (fmeta, fmeta_all)):
        for g in greet[:-1]:
            cp = copy_to(own, all_.at[me], meta_sems, at, **g)
            cp.start()
            meta_copies.append(cp)
            at += 1

    def tiles_of(source, who, part):
        first = (source * 2 + who) * held + part * share
        return tiles_all.at[pl.ds(first, share)]

    tile_sems = (tile_send, tile_recv)
    k3 = owners - 1
    near = f + 1 - 2 * lax.rem(f, 2)
    is_inner = (f == 1) | (f == 2)
    partner = 3 - f
    origin = [near, jnp.where(is_inner, partner, 3 - near), jnp.where(is_inner, 3 - near, partner)]
    own_share = pairs.at[pl.ds(t * share, share)]
    to_near = copy_to(own_share, tiles_of(f, rep, t), tile_sems, 0, fam=near)
    to_near.start()

    def relay(src, owner, send_at, recv_at, to):
        cp = pltpu.make_async_remote_copy(
            src_ref=src,
            dst_ref=tiles_of(owner, rep, t),
            send_sem=relay_send.at[send_at],
            recv_sem=tile_recv.at[recv_at],
            device_id=dict(fam=to),
            device_id_type=pl.DeviceIdType.MESH,
        )
        return cp

    across_mid = jnp.where(is_inner, partner, near)
    relays = [
        relay(own_share, f, 0, 1, across_mid),
        relay(tiles_of(origin[0], rep, t), origin[0], 1, 2, across_mid),
        relay(tiles_of(origin[1], rep, t), origin[1], 2, 1, near),
        relay(tiles_of(origin[2], rep, t), origin[2], 3, 2, near),
    ]

    @pl.when(is_inner)
    def _():
        relays[0].start()

    own_tiles = tiles_all.at[pl.ds(me * held, held)]
    tile_home = copy_to(pairs, own_tiles, tile_sems, 4 * k3, rep=other)
    tile_home.start()

    ph_sems = (ph_send, ph_recv)
    ph_along = []
    for k, p in enumerate(peers):
        cp = copy_to(
            pheno.at[pl.ds(rep * half, half), pl.ds(pl.multiple_of(p * n, n), n)],
            ph_all.at[pl.ds(f * persons + rep * half, half)],
            ph_sems,
            k,
            fam=p,
        )
        cp.start()
        ph_along.append(cp)

    keep = [
        pltpu.make_async_copy(imeta, imeta_all.at[me], local_sem.at[0]),
        pltpu.make_async_copy(fmeta, fmeta_all.at[me], local_sem.at[1]),
        pltpu.make_async_copy(pairs, own_tiles, local_sem.at[2]),
        pltpu.make_async_copy(
            pheno.at[:, pl.ds(pl.multiple_of(f * n, n), n)],
            ph_all.at[pl.ds(f * persons, persons)],
            local_sem.at[3],
        ),
    ]
    for cp in keep:
        cp.start()
    tiles_all[blank] = jnp.zeros(tiles_all.shape[1:], jnp.float32)
    for cp in keep:
        cp.wait()
    for cp in meta_copies:
        cp.wait()

    inv_v[...] = jnp.zeros(inv_v.shape, jnp.int32)
    pos_lane = lax.broadcasted_iota(jnp.int32, (held, n), 1)
    tile_id = lax.broadcasted_iota(jnp.int32, (held, n), 0)
    for o in range(owners):
        found = jnp.zeros((1, n), jnp.int32)
        for q in range(2):
            j = 2 * o + q
            im = imeta_all[j]
            imt = im.T
            at = slice(j * n, (j + 1) * n)
            col_row[:, at] = im[4:5]
            row_row[:, at] = im[5:6]
            col_col[at, :] = imt[:, 4:5]
            row_col[at, :] = imt[:, 5:6]
            fmt = fmeta_all[j].T
            weight[at, :] = fmt[:, 4:5]
            hit = jnp.where(imt[:held, 6:7] == pos_lane, tile_id + (j * held + 1), 0)
            found = jnp.maximum(found, jnp.max(hit, axis=0, keepdims=True))
            if q == 0:
                for i in range(persons // n):
                    at = slice(o * persons + i * n, o * persons + (i + 1) * n)
                    match_row[:, at] = im[i : i + 1]
                    diag[at, :] = fmt[:, i : i + 1]
        inv_v[o : o + 1, :] = jnp.where(found == 0, blank, found - 1)
    to_scalar = pltpu.make_async_copy(inv_v, inv, local_sem.at[4])
    to_scalar.start()

    one_hot_rows(c, col_col, entries, 64)
    one_hot_cols(ct, col_row, every, 64)
    tile_across, tile_side = [], []
    for k, s in enumerate(origin):
        if k == 0:
            to_near.wait()
        else:
            copy_to(own_share, tiles_of(s, rep, t), tile_sems, k, fam=near).wait_recv()

        @pl.when(is_inner)
        def _():
            relays[k + 1].start()

        cp = copy_to(tiles_of(s, rep, t), tiles_of(s, rep, t), tile_sems, k3 + k, trait=across)
        cp.start()
        tile_across.append(cp)
        cp = copy_to(tiles_of(s, rep, t), tiles_of(s, rep, t), tile_sems, 2 * k3 + k, rep=other)
        cp.start()
        tile_side.append(cp)
    one_hot_rows(rsel, row_col, entries, 64)
    for o in range(owners):
        lane = row_row[:, o * eown : (o + 1) * eown]
        sub = lax.broadcasted_iota(jnp.int32, (persons, eown), 0)
        rselt[o] = jnp.where(lane == sub, 1.0, 0.0).astype(jnp.bfloat16)
    for k, s in enumerate(origin):
        tile_across[k].wait()
        part = tiles_of(s, rep, across)
        cp = copy_to(part, part, tile_sems, 3 * k3 + k, rep=other)
        cp.start()
        tile_side.append(cp)
    one_hot_cols(pm, match_row, every, 64)
    to_scalar.wait()
    tile_home.wait()
    for cp in tile_side:
        cp.wait()

    @pl.when(is_inner)
    def _():
        for cp in relays:
            cp.wait_send()


    def factor(o, _):
        for a2 in range(nblk // 2):
            rows = []
            for a in (2 * a2, 2 * a2 + 1):
                got = [tiles_all[inv[o, a * nblk + b]] for b in range(nblk)]
                rows.append(jnp.concatenate([g[:, :64] for g in got], axis=1))
                rows.append(jnp.concatenate([g[:, 64:] for g in got], axis=1))
            full = jnp.concatenate(rows, axis=0)
            at = slice(a2 * 128, (a2 + 1) * 128)
            high = full.astype(jnp.bfloat16)
            khi[o, at, :] = high
            klo[o, at, :] = (full - high.astype(jnp.float32)).astype(jnp.bfloat16)
            full = full.T
            high = full.astype(jnp.bfloat16)
            kthi[o, :, at] = high
            ktlo[o, :, at] = (full - high.astype(jnp.float32)).astype(jnp.bfloat16)
        return 0

    lax.fori_loop(0, owners, factor, 0)

    ph_side = []
    for k, s in enumerate(sources):
        ph_along[k].wait()
        part = ph_all.at[pl.ds(s * persons + rep * half, half)]
        cp = copy_to(part, part, ph_sems, k3 + k, rep=other)
        cp.start()
        ph_side.append(cp)

    def person(o):
        return pl.ds(pl.multiple_of(o * persons, persons), persons)

    def entry(o):
        return pl.ds(pl.multiple_of(o * eown, eown), eown)

    zero = jnp.zeros((1, n), jnp.float32)

    def colsum(v):
        return jnp.sum(v, axis=0, keepdims=True)

    for cp in ph_side:
        cp.wait()
    ycat[...] = split_terms(ph_all[...])

    out_sems = (out_send, out_recv)

    def block(o):
        return pl.ds(pl.multiple_of(o * n, n), n)

    def give(src, dst, k, at):
        cp = copy_to(src.at[pl.ds(peers[k] * persons + rep * half, half)], dst, out_sems, at, fam=peers[k])
        cp.start()
        return cp

    def give_direction(step):
        return [give(d.at[step], got.at[step, :, block(f)], k, step * k3 + k) for k in range(k3)]

    def begin(o, carry):
        rr, dd = carry
        v = fold(mm(pm[person(o), :], ycat[...]))
        r[person(o), :] = v
        d[0, person(o), :] = v
        dcat[person(o), :] = split_terms(v)
        square = v * v
        return rr + colsum(square), dd + colsum(square * diag[person(o), :])

    rr, dd = lax.fori_loop(0, owners, begin, (zero, zero))
    given = give_direction(0)

    def forward(o, yy):
        g = fold(mm(c[entry(o), :], dcat[...])) * weight[entry(o), :]
        near = dcat[person(o), :]
        y = fold(mm(khi[o], near) + mm(rselt[o], split_terms(g)))
        y = y + mm(klo[o], near[:, :n])
        ys = split_terms(y)
        ycat[person(o), :] = ys
        h = fold(mm(rsel[entry(o), :], ys)) * weight[entry(o), :]
        hcat[entry(o), :] = split_terms(h)
        return yy + colsum(y * y)

    def image(o, step):
        ys = ycat[person(o), :]
        back = fold(mm(kthi[o], ys) + mm(ct[person(o), :], hcat[...]))
        back = back + mm(ktlo[o], ys[:, :n])
        return diag[person(o), :] * d[step, person(o), :] + back

    for step in range(ITERS - 1):
        yy = lax.fori_loop(0, owners, forward, zero)
        alpha = rr / (yy + dd)
        al[step : step + 1, :] = alpha

        def descend(o, acc):
            left = r[person(o), :] - alpha * image(o, step)
            r[person(o), :] = left
            return acc + colsum(left * left)

        nxt = lax.fori_loop(0, owners, descend, zero)
        beta = nxt / rr
        rr = nxt

        def turn(o, acc):
            v = r[person(o), :] + beta * d[step, person(o), :]
            d[step + 1, person(o), :] = v
            dcat[person(o), :] = split_terms(v)
            return acc + colsum(v * v * diag[person(o), :])

        dd = lax.fori_loop(0, owners, turn, zero)
        given += give_direction(step + 1)

    last = ITERS - 1
    yy = lax.fori_loop(0, owners, forward, zero)
    alpha = rr / (yy + dd)
    al[last : last + 1, :] = alpha
    base = ITERS * k3
    told = []
    for k in range(k3):
        cp = copy_to(al, al_all.at[f], out_sems, base + k, fam=peers[k])
        cp.start()
        told.append(cp)

    mine = pl.ds(rep * half, half)
    theirs = []
    for k in range(owners):
        o = peers[k] if k < k3 else f
        r[person(o), :] = r[person(o), :] - alpha * image(o, last)
        if k < k3:
            theirs.append(give(r, r_out.at[mine, block(f)], k, base + k3 + k))
    stay = pltpu.make_async_copy(
        r.at[pl.ds(f * persons, persons)], r_out.at[:, block(f)], local_sem.at[5]
    )
    stay.start()
    for cp in given + told:
        cp.wait()

    home = pl.ds(f * persons + rep * half, half)
    total = al[0:1, :] * d[0, home, :]
    for u in range(1, ITERS):
        total = total + al[u : u + 1, :] * d[u, home, :]
    x_out[mine, block(f)] = total
    for s in sources:
        total = al_all[s, 0:1, :] * got[0, :, block(s)]
        for u in range(1, ITERS):
            total = total + al_all[s, u : u + 1, :] * got[u, :, block(s)]
        x_out[mine, block(s)] = total
    side = [copy_to(x_out.at[mine], x_out.at[mine], out_sems, base + 2 * k3, rep=other)]
    side[0].start()
    for i, cp in enumerate(theirs):
        cp.wait()
        part = r_out.at[mine, block(sources[i])]
        cp = copy_to(part, part, out_sems, base + 2 * k3 + 1 + i, rep=other)
        cp.start()
        side.append(cp)
    for cp in side + [stay]:
        cp.wait()


def local_group(
    pheno,
    match,
    diag_var,
    tiles,
    tile_row_family,
    tile_cols,
    rel_row,
    rel_peer,
    rel_slot,
    rel_weight,
):
    owners = lax.axis_size("fam")
    persons, columns = pheno.shape
    n = columns // owners
    held = tiles.shape[0]
    lists = 2 * owners
    every = owners * persons
    entries = lists * rel_row.shape[0]
    eown = entries // owners
    vmem = pl.BlockSpec(memory_space=pltpu.VMEM)
    bf, f32, i32 = jnp.bfloat16, jnp.float32, jnp.int32
    k3 = owners - 1
    dma = pltpu.SemaphoreType.DMA
    return pl.pallas_call(
        functools.partial(group_kernel, owners),
        out_shape=[jax.ShapeDtypeStruct((persons, columns), f32)] * 2,
        in_specs=[vmem] * 10,
        out_specs=[vmem] * 2,
        scratch_shapes=[
            pltpu.VMEM((8, n), i32),
            pltpu.VMEM((8, n), f32),
            pltpu.VMEM((held, 32, 128), f32),
            pltpu.VMEM((lists, 8, n), i32),
            pltpu.VMEM((lists, 8, n), f32),
            pltpu.VMEM((lists * held + 1, 32, 128), f32),
            pltpu.VMEM((every, n), f32),
            pltpu.VMEM((8, n), i32),
            pltpu.SMEM((8, n), i32),
            pltpu.VMEM((1, every), i32),
            pltpu.VMEM((1, entries), i32),
            pltpu.VMEM((1, entries), i32),
            pltpu.VMEM((entries, 1), i32),
            pltpu.VMEM((entries, 1), i32),
            pltpu.VMEM((entries, 1), f32),
            pltpu.VMEM((every, 1), f32),
            pltpu.VMEM((owners, persons, persons), bf),
            pltpu.VMEM((owners, persons, persons), bf),
            pltpu.VMEM((owners, persons, persons), bf),
            pltpu.VMEM((owners, persons, persons), bf),
            pltpu.VMEM((every, every), bf),
            pltpu.VMEM((entries, every), bf),
            pltpu.VMEM((every, entries), bf),
            pltpu.VMEM((entries, persons), bf),
            pltpu.VMEM((owners, persons, eown), bf),
            pltpu.VMEM((ITERS, every, n), f32),
            pltpu.VMEM((every, n), f32),
            pltpu.VMEM((ITERS, persons // 2, columns), f32),
            pltpu.VMEM((8, n), f32),
            pltpu.VMEM((owners, 8, n), f32),
            pltpu.VMEM((every, 2 * n), bf),
            pltpu.VMEM((every, 2 * n), bf),
            pltpu.VMEM((entries, 2 * n), bf),
            dma((2 * lists - 2,)),
            dma((2 * lists - 2,)),
            dma((4 * k3 + 1,)),
            dma((4 * k3 + 1,)),
            dma((2 * k3,)),
            dma((2 * k3,)),
            dma(((ITERS + 3) * k3 + 1,)),
            dma(((ITERS + 3) * k3 + 1,)),
            dma((4,)),
            dma((7,)),
        ],
        compiler_params=pltpu.CompilerParams(
            vmem_limit_bytes=60 * 2**20, collective_id=0, has_side_effects=True
        ),
    )(
        match.reshape(-1, n),
        diag_var.reshape(-1, n),
        tiles,
        tile_row_family.reshape(1, -1),
        tile_cols.reshape(1, -1),
        rel_row.reshape(1, -1),
        rel_peer.reshape(1, -1),
        rel_slot.reshape(1, -1),
        rel_weight.reshape(1, -1),
        pheno,
    )


def solution(mesh):
    placed = (
        P(("groups", "fam"), "trait"),
        P(("groups", "fam")),
        P(("groups", "fam")),
        P(("groups", "fam", "rep"), None),
        P(("groups", "fam", "rep")),
        P(("groups", "fam", "rep")),
        P(("groups", "fam", "rep")),
        P(("groups", "fam", "rep"), None),
        P(("groups", "fam", "rep")),
        P(("groups", "fam", "rep")),
    )
    whole = mesh.shape["fam"] == 4 and mesh.shape["trait"] == 2 and mesh.shape["rep"] == 2
    return jax.shard_map(
        local_group if whole else local,
        mesh=mesh,
        in_specs=placed,
        out_specs=(P(("groups", "fam"), "trait"), P(("groups", "fam"), "trait")),
        check_vma=False,
    )
```

```python
import functools

import jax
import jax.numpy as jnp
from jax import lax
from jax.experimental import pallas as pl
from jax.experimental.pallas import tpu as pltpu
from jax.sharding import PartitionSpec as P

ITERS = 3


PRECISION_HIGH = lax.Precision.HIGHEST


def block_rank(owner, groups):
    marker_flags = (owner[:, None] == jnp.arange(groups, dtype=jnp.int32)[None, :]).astype(
        jnp.int32
    )
    ranks = jnp.cumsum(marker_flags, axis=0) - 1
    return jnp.sum(ranks * marker_flags, axis=1)


def forward_tile_map(solution_values, tiles, trow, tcol, nblocks):
    blocks = solution_values.reshape(nblocks, 64, solution_values.shape[1])
    selected_entries = blocks[tcol]
    operator_products = jnp.einsum(
        "olh,ohj->olj", tiles, selected_entries, precision=PRECISION_HIGH
    )
    marker_flags = (trow[None, :] == jnp.arange(nblocks, dtype=jnp.int32)[:, None]).astype(
        jnp.float32
    )
    return jnp.einsum(
        "fo,ouh->fuh", marker_flags, operator_products, precision=PRECISION_HIGH
    ).reshape(solution_values.shape)


def tile_backward(solution_values, tiles, trow, tcol, nblocks):
    blocks = solution_values.reshape(nblocks, 64, solution_values.shape[1])
    selected_entries = blocks[trow]
    operator_products = jnp.einsum(
        "zxp,zxm->zpm", tiles, selected_entries, precision=PRECISION_HIGH
    )
    marker_flags = (tcol[None, :] == jnp.arange(nblocks, dtype=jnp.int32)[:, None]).astype(
        jnp.float32
    )
    return jnp.einsum(
        "fo,ouh->fuh", marker_flags, operator_products, precision=PRECISION_HIGH
    ).reshape(solution_values.shape)


def total_squares(solution_values):
    return lax.psum(jnp.sum(solution_values * solution_values, axis=0), "fam")


def local(
    pheno,
    match,
    diag_var,
    tiles,
    tile_row_family,
    tile_cols,
    rel_row,
    rel_peer,
    rel_slot,
    rel_weight,
):
    groups = lax.axis_size("fam")
    persons = pheno.shape[0]
    nblocks = persons // 64
    tile_set = tiles.reshape(tiles.shape[0], 64, 64)
    peers = rel_peer[:, 0]
    weights = rel_weight[:, None]
    columns = pheno.shape[1]
    owner = match // persons
    slot = match % persons
    cap = 2 * persons // groups
    dest = owner * cap + block_rank(owner, groups)
    send_vals = jnp.zeros((groups * cap, columns), jnp.float32).at[dest].set(pheno)
    send_slots = jnp.full((groups * cap,), -1.0, jnp.float32).at[dest].set(slot.astype(jnp.float32))
    got_vals, got_slots = (
        lax.all_to_all(send_vals, "fam", split_axis=0, concat_axis=0, tiled=True),
        lax.all_to_all(send_slots, "fam", split_axis=0, concat_axis=0, tiled=True),
    )
    landing = jnp.where(got_slots >= 0, got_slots.astype(jnp.int32), persons)
    target = jnp.zeros((persons, columns), jnp.float32).at[landing].set(got_vals, mode="drop")
    entries = rel_row.shape[0]
    rcap = 2 * entries // groups
    rdest = peers * rcap + block_rank(peers, groups)
    asks = jnp.full((groups * rcap,), -1, jnp.int32).at[rdest].set(rel_slot)
    incoming = lax.all_to_all(asks, "fam", split_axis=0, concat_axis=0, tiled=True)
    valid = incoming >= 0
    picked_slot = jnp.where(valid, incoming, 0)
    arriving = jnp.where(valid, incoming, persons)
    solution_field = jnp.zeros((persons, columns), jnp.float32)
    residual = target
    direction = target
    norm_now = total_squares(residual)
    for step in range(ITERS):
        factor_part = forward_tile_map(direction, tile_set, tile_row_family, tile_cols, nblocks)
        outgoing = jnp.where(valid[:, None], direction[picked_slot], 0.0)
        answers = lax.all_to_all(outgoing, "fam", split_axis=0, concat_axis=0, tiled=True)
        factor_part = factor_part.at[rel_row].add(weights * answers[rdest])
        factor_part = lax.psum(factor_part, "rep")
        part = tile_backward(factor_part, tile_set, tile_row_family, tile_cols, nblocks)
        pushed = (
            jnp.zeros((groups * rcap, columns), jnp.float32)
            .at[rdest]
            .set(weights * factor_part[rel_row])
        )
        landed = lax.all_to_all(pushed, "fam", split_axis=0, concat_axis=0, tiled=True)
        part = part.at[arriving].add(landed, mode="drop")
        part = lax.psum(part, "rep")
        image = diag_var[:, None] * direction + part
        curvature = lax.psum(jnp.sum(direction * image, axis=0), "fam")
        alpha = norm_now / curvature
        solution_field = solution_field + alpha[None, :] * direction
        residual = residual - alpha[None, :] * image
        norm_next = total_squares(residual)
        direction = residual + (norm_next / norm_now)[None, :] * direction
        norm_now = norm_next
    return (solution_field, residual)


def split_terms(values):
    high = values.astype(jnp.bfloat16)
    low = (values - high.astype(jnp.float32)).astype(jnp.bfloat16)
    return jnp.concatenate([high, low], axis=1)


def fold(values):
    half = values.shape[1] // 2
    return values[:, :half] + values[:, half:]


def mm(left, right):
    return jnp.dot(left, right, preferred_element_type=jnp.float32)


def one_hot_rows(ref, index_col, rows, strip):
    width = ref.shape[1]

    def body(i, _):
        at = pl.ds(pl.multiple_of(i * strip, strip), strip)
        lane = lax.broadcasted_iota(jnp.int32, (strip, width), 1)
        ref[at, :] = jnp.where(index_col[at, :] == lane, 1.0, 0.0).astype(jnp.bfloat16)
        return 0

    lax.fori_loop(0, rows // strip, body, 0)


def one_hot_cols(ref, index_row, rows, strip):
    width = ref.shape[1]

    def body(i, _):
        at = pl.ds(pl.multiple_of(i * strip, strip), strip)
        sub = lax.broadcasted_iota(jnp.int32, (strip, width), 0) + i * strip
        ref[at, :] = jnp.where(index_row[...] == sub, 1.0, 0.0).astype(jnp.bfloat16)
        return 0

    lax.fori_loop(0, rows // strip, body, 0)


def copy_to(src, dst, sems, at, **where):
    send, recv = sems
    return pltpu.make_async_remote_copy(
        src_ref=src,
        dst_ref=dst,
        send_sem=send.at[at],
        recv_sem=recv.at[at],
        device_id=where,
        device_id_type=pl.DeviceIdType.MESH,
    )


def group_kernel(
    owners,
    match,
    diag_own,
    tiles,
    trow,
    tcol,
    rel_row,
    rel_peer,
    rel_slot,
    rel_weight,
    pheno,
    x_out,
    r_out,
    imeta,
    fmeta,
    pairs,
    imeta_all,
    fmeta_all,
    tiles_all,
    ph_all,
    inv_v,
    inv,
    match_row,
    col_row,
    row_row,
    col_col,
    row_col,
    weight,
    diag,
    khi,
    klo,
    kthi,
    ktlo,
    pm,
    c,
    ct,
    rsel,
    rselt,
    d,
    r,
    xs,
    got,
    al,
    al_all,
    dcat,
    ycat,
    hcat,
    meta_send,
    meta_recv,
    tile_send,
    tile_recv,
    ph_send,
    ph_recv,
    out_send,
    out_recv,
    local_sem,
):
    persons = pheno.shape[0]
    every = owners * persons
    entries = c.shape[0]
    eown = entries // owners
    n = r.shape[1]
    held = pairs.shape[0]
    share = held // 2
    half = persons // 2
    nblk = persons // 64
    lists = 2 * owners
    blank = lists * held
    f = lax.axis_index("fam")
    t = lax.axis_index("trait")
    rep = lax.axis_index("rep")
    other = 1 - rep
    across = 1 - t
    me = f * 2 + rep
    peers = [lax.rem(f + k, owners) for k in range(1, owners)]
    sources = [lax.rem(f + owners - k, owners) for k in range(1, owners)]

    barrier = pltpu.get_barrier_semaphore()
    greet = [dict(fam=p, rep=q) for p in peers for q in (rep, other)]
    greet += [dict(rep=other), dict(trait=across)]
    for g in greet:
        pl.semaphore_signal(barrier, inc=1, device_id=g, device_id_type=pl.DeviceIdType.MESH)

    inner = rel_row[...] % 64
    imeta[...] = jnp.full(imeta.shape, -1, jnp.int32)
    fmeta[...] = jnp.zeros(fmeta.shape, jnp.float32)
    imeta[0 : persons // n, :] = match[...]
    imeta[4:5, :] = rel_peer[...] * persons + rel_slot[...]
    imeta[5:6, :] = rel_row[...] - inner + (inner % 2) * 32 + inner // 2
    imeta[6:7, 0:held] = trow[...] * nblk + tcol[...]
    fmeta[0 : persons // n, :] = diag_own[...]
    fmeta[4:5, :] = rel_weight[...]
    for i in range(32):
        pairs[:, i, :] = tiles[:, i * 128 : (i + 1) * 128]
    pl.semaphore_wait(barrier, len(greet))

    meta_sems = (meta_send, meta_recv)
    meta_copies = []
    at = 0
    for own, all_ in ((imeta, imeta_all), (fmeta, fmeta_all)):
        for g in greet[:-1]:
            cp = copy_to(own, all_.at[me], meta_sems, at, **g)
            cp.start()
            meta_copies.append(cp)
            at += 1

    def tiles_of(source, who, part):
        first = (source * 2 + who) * held + part * share
        return tiles_all.at[pl.ds(first, share)]

    tile_sems = (tile_send, tile_recv)
    k3 = owners - 1
    along = []
    for k, p in enumerate(peers):
        cp = copy_to(pairs.at[pl.ds(t * share, share)], tiles_of(f, rep, t), tile_sems, k, fam=p)
        cp.start()
        along.append(cp)
    own_tiles = tiles_all.at[pl.ds(me * held, held)]
    tile_home = copy_to(pairs, own_tiles, tile_sems, 4 * k3, rep=other)
    tile_home.start()

    keep = [
        pltpu.make_async_copy(imeta, imeta_all.at[me], local_sem.at[0]),
        pltpu.make_async_copy(fmeta, fmeta_all.at[me], local_sem.at[1]),
        pltpu.make_async_copy(pairs, own_tiles, local_sem.at[2]),
        pltpu.make_async_copy(
            pheno.at[:, pl.ds(pl.multiple_of(f * n, n), n)],
            ph_all.at[pl.ds(f * persons, persons)],
            local_sem.at[3],
        ),
    ]
    for cp in keep:
        cp.start()
    tiles_all[blank] = jnp.zeros(tiles_all.shape[1:], jnp.float32)
    for cp in keep:
        cp.wait()
    for cp in meta_copies:
        cp.wait()

    inv_v[...] = jnp.zeros(inv_v.shape, jnp.int32)
    pos_lane = lax.broadcasted_iota(jnp.int32, (held, n), 1)
    tile_id = lax.broadcasted_iota(jnp.int32, (held, n), 0)
    for o in range(owners):
        found = jnp.zeros((1, n), jnp.int32)
        for q in range(2):
            j = 2 * o + q
            im = imeta_all[j]
            imt = im.T
            at = slice(j * n, (j + 1) * n)
            col_row[:, at] = im[4:5]
            row_row[:, at] = im[5:6]
            col_col[at, :] = imt[:, 4:5]
            row_col[at, :] = imt[:, 5:6]
            fmt = fmeta_all[j].T
            weight[at, :] = fmt[:, 4:5]
            hit = jnp.where(imt[:held, 6:7] == pos_lane, tile_id + (j * held + 1), 0)
            found = jnp.maximum(found, jnp.max(hit, axis=0, keepdims=True))
            if q == 0:
                for i in range(persons // n):
                    at = slice(o * persons + i * n, o * persons + (i + 1) * n)
                    match_row[:, at] = im[i : i + 1]
                    diag[at, :] = fmt[:, i : i + 1]
        inv_v[o : o + 1, :] = jnp.where(found == 0, blank, found - 1)
    to_scalar = pltpu.make_async_copy(inv_v, inv, local_sem.at[4])
    to_scalar.start()

    tile_across, tile_side = [], []
    for k, s in enumerate(sources):
        along[k].wait()
        cp = copy_to(tiles_of(s, rep, t), tiles_of(s, rep, t), tile_sems, k3 + k, trait=across)
        cp.start()
        tile_across.append(cp)
        cp = copy_to(tiles_of(s, rep, t), tiles_of(s, rep, t), tile_sems, 2 * k3 + k, rep=other)
        cp.start()
        tile_side.append(cp)
    ph_sems = (ph_send, ph_recv)
    ph_along = []
    for k, p in enumerate(peers):
        cp = copy_to(
            pheno.at[pl.ds(rep * half, half), pl.ds(pl.multiple_of(p * n, n), n)],
            ph_all.at[pl.ds(f * persons + rep * half, half)],
            ph_sems,
            k,
            fam=p,
        )
        cp.start()
        ph_along.append(cp)

    one_hot_rows(rsel, row_col, entries, 64)
    for o in range(owners):
        lane = row_row[:, o * eown : (o + 1) * eown]
        sub = lax.broadcasted_iota(jnp.int32, (persons, eown), 0)
        rselt[o] = jnp.where(lane == sub, 1.0, 0.0).astype(jnp.bfloat16)
    for k, s in enumerate(sources):
        tile_across[k].wait()
        part = tiles_of(s, rep, across)
        cp = copy_to(part, part, tile_sems, 3 * k3 + k, rep=other)
        cp.start()
        tile_side.append(cp)
    one_hot_rows(c, col_col, entries, 64)
    one_hot_cols(ct, col_row, every, 64)
    one_hot_cols(pm, match_row, every, 64)
    to_scalar.wait()
    tile_home.wait()
    for cp in tile_side:
        cp.wait()

    def factor(o, _):
        for a2 in range(nblk // 2):
            rows = []
            for a in (2 * a2, 2 * a2 + 1):
                got = [tiles_all[inv[o, a * nblk + b]] for b in range(nblk)]
                rows.append(jnp.concatenate([g[:, :64] for g in got], axis=1))
                rows.append(jnp.concatenate([g[:, 64:] for g in got], axis=1))
            full = jnp.concatenate(rows, axis=0)
            at = slice(a2 * 128, (a2 + 1) * 128)
            high = full.astype(jnp.bfloat16)
            khi[o, at, :] = high
            klo[o, at, :] = (full - high.astype(jnp.float32)).astype(jnp.bfloat16)
            full = full.T
            high = full.astype(jnp.bfloat16)
            kthi[o, :, at] = high
            ktlo[o, :, at] = (full - high.astype(jnp.float32)).astype(jnp.bfloat16)
        return 0

    lax.fori_loop(0, owners, factor, 0)

    ph_side = []
    for k, s in enumerate(sources):
        ph_along[k].wait()
        part = ph_all.at[pl.ds(s * persons + rep * half, half)]
        cp = copy_to(part, part, ph_sems, k3 + k, rep=other)
        cp.start()
        ph_side.append(cp)

    def person(o):
        return pl.ds(pl.multiple_of(o * persons, persons), persons)

    def entry(o):
        return pl.ds(pl.multiple_of(o * eown, eown), eown)

    zero = jnp.zeros((1, n), jnp.float32)

    def colsum(v):
        return jnp.sum(v, axis=0, keepdims=True)

    for cp in ph_side:
        cp.wait()
    ycat[...] = split_terms(ph_all[...])

    out_sems = (out_send, out_recv)

    def block(o):
        return pl.ds(pl.multiple_of(o * n, n), n)

    early = half // 2

    def rows_of(o, first, count):
        return pl.ds(pl.multiple_of(o * persons + rep * half + first, early), count)

    def give(src, first, count, dst, k, unit):
        part = src.at[rows_of(peers[k], first, count)]
        cp = copy_to(part, dst, out_sems, unit * k3 + k, fam=peers[k])
        cp.start()
        return cp

    def give_early(src, which):
        return [give(src, 0, early, got.at[which, :, block(f)], k, which) for k in range(k3)]

    def begin(o, carry):
        rr, dd = carry
        v = fold(mm(pm[person(o), :], ycat[...]))
        r[person(o), :] = v
        d[0, person(o), :] = v
        dcat[person(o), :] = split_terms(v)
        square = v * v
        return rr + colsum(square), dd + colsum(square * diag[person(o), :])

    rr, dd = lax.fori_loop(0, owners, begin, (zero, zero), unroll=True)
    given = []

    def forward(o, yy):
        g = fold(mm(c[entry(o), :], dcat[...])) * weight[entry(o), :]
        near = dcat[person(o), :]
        y = fold(mm(khi[o], near) + mm(rselt[o], split_terms(g)))
        y = y + mm(klo[o], near[:, :n])
        ys = split_terms(y)
        ycat[person(o), :] = ys
        h = fold(mm(rsel[entry(o), :], ys)) * weight[entry(o), :]
        hcat[entry(o), :] = split_terms(h)
        return yy + colsum(y * y)

    def image(o, step):
        ys = ycat[person(o), :]
        back = fold(mm(kthi[o], ys) + mm(ct[person(o), :], hcat[...]))
        back = back + mm(ktlo[o], ys[:, :n])
        return diag[person(o), :] * d[step, person(o), :] + back

    for step in range(ITERS - 1):
        yy = lax.fori_loop(0, owners, forward, zero, unroll=True)
        alpha = rr / (yy + dd)
        for o in range(owners):
            at = slice(o * persons, (o + 1) * persons)
            move = alpha * d[step, at, :]
            xs[at, :] = move if step == 0 else xs[at, :] + move
        if step == ITERS - 2:
            given += give_early(xs, 0)

        def descend(o, acc):
            left = r[person(o), :] - alpha * image(o, step)
            r[person(o), :] = left
            return acc + colsum(left * left)

        nxt = lax.fori_loop(0, owners, descend, zero, unroll=True)
        beta = nxt / rr
        rr = nxt

        def turn(o, acc):
            v = r[person(o), :] + beta * d[step, person(o), :]
            d[step + 1, person(o), :] = v
            dcat[person(o), :] = split_terms(v)
            return acc + colsum(v * v * diag[person(o), :])

        dd = lax.fori_loop(0, owners, turn, zero, unroll=True)

    last = ITERS - 1
    given += give_early(d.at[last], 1)
    yy = lax.fori_loop(0, owners, forward, zero, unroll=True)
    alpha = rr / (yy + dd)
    al[0:1, :] = alpha
    for k in range(k3):
        cp = copy_to(al, al_all.at[f], out_sems, 2 * k3 + k, fam=peers[k])
        cp.start()
        given.append(cp)

    mine = pl.ds(rep * half, half)
    mine_early = pl.ds(rep * half, early)
    mine_late = pl.ds(rep * half + early, half - early)
    for k in range(k3):
        at = rows_of(peers[k], early, half - early)
        xs[at, :] = xs[at, :] + alpha * d[last, at, :]
        given.append(give(xs, early, half - early, x_out.at[mine_late, block(f)], k, 3))
    theirs = []
    for k in range(owners):
        o = peers[k] if k < k3 else f
        r[person(o), :] = r[person(o), :] - alpha * image(o, last)
        if k < k3:
            theirs.append(give(r, 0, half, r_out.at[mine, block(f)], k, 4))
    stay = pltpu.make_async_copy(
        r.at[pl.ds(f * persons, persons)], r_out.at[:, block(f)], local_sem.at[5]
    )
    stay.start()
    for cp in given:
        cp.wait()

    home = rows_of(f, 0, half)
    x_out[mine, block(f)] = xs[home, :] + alpha * d[last, home, :]
    for s in sources:
        x_out[mine_early, block(s)] = got[0, :, block(s)] + al_all[s, 0:1, :] * got[1, :, block(s)]
    base = 5 * k3
    side = [copy_to(x_out.at[mine], x_out.at[mine], out_sems, base, rep=other)]
    side[0].start()
    for i, cp in enumerate(theirs):
        cp.wait()
        part = r_out.at[mine, block(sources[i])]
        cp = copy_to(part, part, out_sems, base + 1 + i, rep=other)
        cp.start()
        side.append(cp)
    for cp in side + [stay]:
        cp.wait()


def local_group(
    pheno,
    match,
    diag_var,
    tiles,
    tile_row_family,
    tile_cols,
    rel_row,
    rel_peer,
    rel_slot,
    rel_weight,
):
    owners = lax.axis_size("fam")
    persons, columns = pheno.shape
    n = columns // owners
    held = tiles.shape[0]
    lists = 2 * owners
    every = owners * persons
    entries = lists * rel_row.shape[0]
    eown = entries // owners
    vmem = pl.BlockSpec(memory_space=pltpu.VMEM)
    bf, f32, i32 = jnp.bfloat16, jnp.float32, jnp.int32
    k3 = owners - 1
    dma = pltpu.SemaphoreType.DMA
    return pl.pallas_call(
        functools.partial(group_kernel, owners),
        out_shape=[jax.ShapeDtypeStruct((persons, columns), f32)] * 2,
        in_specs=[vmem] * 10,
        out_specs=[vmem] * 2,
        scratch_shapes=[
            pltpu.VMEM((8, n), i32),
            pltpu.VMEM((8, n), f32),
            pltpu.VMEM((held, 32, 128), f32),
            pltpu.VMEM((lists, 8, n), i32),
            pltpu.VMEM((lists, 8, n), f32),
            pltpu.VMEM((lists * held + 1, 32, 128), f32),
            pltpu.VMEM((every, n), f32),
            pltpu.VMEM((8, n), i32),
            pltpu.SMEM((8, n), i32),
            pltpu.VMEM((1, every), i32),
            pltpu.VMEM((1, entries), i32),
            pltpu.VMEM((1, entries), i32),
            pltpu.VMEM((entries, 1), i32),
            pltpu.VMEM((entries, 1), i32),
            pltpu.VMEM((entries, 1), f32),
            pltpu.VMEM((every, 1), f32),
            pltpu.VMEM((owners, persons, persons), bf),
            pltpu.VMEM((owners, persons, persons), bf),
            pltpu.VMEM((owners, persons, persons), bf),
            pltpu.VMEM((owners, persons, persons), bf),
            pltpu.VMEM((every, every), bf),
            pltpu.VMEM((entries, every), bf),
            pltpu.VMEM((every, entries), bf),
            pltpu.VMEM((entries, persons), bf),
            pltpu.VMEM((owners, persons, eown), bf),
            pltpu.VMEM((ITERS, every, n), f32),
            pltpu.VMEM((every, n), f32),
            pltpu.VMEM((every, n), f32),
            pltpu.VMEM((2, persons // 4, columns), f32),
            pltpu.VMEM((8, n), f32),
            pltpu.VMEM((owners, 8, n), f32),
            pltpu.VMEM((every, 2 * n), bf),
            pltpu.VMEM((every, 2 * n), bf),
            pltpu.VMEM((entries, 2 * n), bf),
            dma((2 * lists - 2,)),
            dma((2 * lists - 2,)),
            dma((4 * k3 + 1,)),
            dma((4 * k3 + 1,)),
            dma((2 * k3,)),
            dma((2 * k3,)),
            dma((6 * k3 + 1,)),
            dma((6 * k3 + 1,)),
            dma((7,)),
        ],
        compiler_params=pltpu.CompilerParams(
            vmem_limit_bytes=60 * 2**20, collective_id=0, has_side_effects=True
        ),
    )(
        match.reshape(-1, n),
        diag_var.reshape(-1, n),
        tiles,
        tile_row_family.reshape(1, -1),
        tile_cols.reshape(1, -1),
        rel_row.reshape(1, -1),
        rel_peer.reshape(1, -1),
        rel_slot.reshape(1, -1),
        rel_weight.reshape(1, -1),
        pheno,
    )


def solution(mesh):
    placed = (
        P(("groups", "fam"), "trait"),
        P(("groups", "fam")),
        P(("groups", "fam")),
        P(("groups", "fam", "rep"), None),
        P(("groups", "fam", "rep")),
        P(("groups", "fam", "rep")),
        P(("groups", "fam", "rep")),
        P(("groups", "fam", "rep"), None),
        P(("groups", "fam", "rep")),
        P(("groups", "fam", "rep")),
    )
    whole = mesh.shape["fam"] == 4 and mesh.shape["trait"] == 2 and mesh.shape["rep"] == 2
    return jax.shard_map(
        local_group if whole else local,
        mesh=mesh,
        in_specs=placed,
        out_specs=(P(("groups", "fam"), "trait"), P(("groups", "fam"), "trait")),
        check_vma=False,
    )
```

```python
import functools

import jax
import jax.numpy as jnp
from jax import lax
from jax.experimental import pallas as pl
from jax.experimental.pallas import tpu as pltpu
from jax.sharding import PartitionSpec as P

ITERS = 3


PRECISION_HIGH = lax.Precision.HIGHEST


def block_rank(owner, groups):
    marker_flags = (owner[:, None] == jnp.arange(groups, dtype=jnp.int32)[None, :]).astype(
        jnp.int32
    )
    ranks = jnp.cumsum(marker_flags, axis=0) - 1
    return jnp.sum(ranks * marker_flags, axis=1)


def forward_tile_map(solution_values, tiles, trow, tcol, nblocks):
    blocks = solution_values.reshape(nblocks, 64, solution_values.shape[1])
    selected_entries = blocks[tcol]
    operator_products = jnp.einsum(
        "olh,ohj->olj", tiles, selected_entries, precision=PRECISION_HIGH
    )
    marker_flags = (trow[None, :] == jnp.arange(nblocks, dtype=jnp.int32)[:, None]).astype(
        jnp.float32
    )
    return jnp.einsum(
        "fo,ouh->fuh", marker_flags, operator_products, precision=PRECISION_HIGH
    ).reshape(solution_values.shape)


def tile_backward(solution_values, tiles, trow, tcol, nblocks):
    blocks = solution_values.reshape(nblocks, 64, solution_values.shape[1])
    selected_entries = blocks[trow]
    operator_products = jnp.einsum(
        "zxp,zxm->zpm", tiles, selected_entries, precision=PRECISION_HIGH
    )
    marker_flags = (tcol[None, :] == jnp.arange(nblocks, dtype=jnp.int32)[:, None]).astype(
        jnp.float32
    )
    return jnp.einsum(
        "fo,ouh->fuh", marker_flags, operator_products, precision=PRECISION_HIGH
    ).reshape(solution_values.shape)


def total_squares(solution_values):
    return lax.psum(jnp.sum(solution_values * solution_values, axis=0), "fam")


def local(
    pheno,
    match,
    diag_var,
    tiles,
    tile_row_family,
    tile_cols,
    rel_row,
    rel_peer,
    rel_slot,
    rel_weight,
):
    groups = lax.axis_size("fam")
    persons = pheno.shape[0]
    nblocks = persons // 64
    tile_set = tiles.reshape(tiles.shape[0], 64, 64)
    peers = rel_peer[:, 0]
    weights = rel_weight[:, None]
    columns = pheno.shape[1]
    owner = match // persons
    slot = match % persons
    cap = 2 * persons // groups
    dest = owner * cap + block_rank(owner, groups)
    send_vals = jnp.zeros((groups * cap, columns), jnp.float32).at[dest].set(pheno)
    send_slots = jnp.full((groups * cap,), -1.0, jnp.float32).at[dest].set(slot.astype(jnp.float32))
    got_vals, got_slots = (
        lax.all_to_all(send_vals, "fam", split_axis=0, concat_axis=0, tiled=True),
        lax.all_to_all(send_slots, "fam", split_axis=0, concat_axis=0, tiled=True),
    )
    landing = jnp.where(got_slots >= 0, got_slots.astype(jnp.int32), persons)
    target = jnp.zeros((persons, columns), jnp.float32).at[landing].set(got_vals, mode="drop")
    entries = rel_row.shape[0]
    rcap = 2 * entries // groups
    rdest = peers * rcap + block_rank(peers, groups)
    asks = jnp.full((groups * rcap,), -1, jnp.int32).at[rdest].set(rel_slot)
    incoming = lax.all_to_all(asks, "fam", split_axis=0, concat_axis=0, tiled=True)
    valid = incoming >= 0
    picked_slot = jnp.where(valid, incoming, 0)
    arriving = jnp.where(valid, incoming, persons)
    solution_field = jnp.zeros((persons, columns), jnp.float32)
    residual = target
    direction = target
    norm_now = total_squares(residual)
    for step in range(ITERS):
        factor_part = forward_tile_map(direction, tile_set, tile_row_family, tile_cols, nblocks)
        outgoing = jnp.where(valid[:, None], direction[picked_slot], 0.0)
        answers = lax.all_to_all(outgoing, "fam", split_axis=0, concat_axis=0, tiled=True)
        factor_part = factor_part.at[rel_row].add(weights * answers[rdest])
        factor_part = lax.psum(factor_part, "rep")
        part = tile_backward(factor_part, tile_set, tile_row_family, tile_cols, nblocks)
        pushed = (
            jnp.zeros((groups * rcap, columns), jnp.float32)
            .at[rdest]
            .set(weights * factor_part[rel_row])
        )
        landed = lax.all_to_all(pushed, "fam", split_axis=0, concat_axis=0, tiled=True)
        part = part.at[arriving].add(landed, mode="drop")
        part = lax.psum(part, "rep")
        image = diag_var[:, None] * direction + part
        curvature = lax.psum(jnp.sum(direction * image, axis=0), "fam")
        alpha = norm_now / curvature
        solution_field = solution_field + alpha[None, :] * direction
        residual = residual - alpha[None, :] * image
        norm_next = total_squares(residual)
        direction = residual + (norm_next / norm_now)[None, :] * direction
        norm_now = norm_next
    return (solution_field, residual)


def split_terms(values):
    high = values.astype(jnp.bfloat16)
    low = (values - high.astype(jnp.float32)).astype(jnp.bfloat16)
    return jnp.concatenate([high, low], axis=1)


def fold(values):
    half = values.shape[1] // 2
    return values[:, :half] + values[:, half:]


def mm(left, right):
    return jnp.dot(left, right, preferred_element_type=jnp.float32)


def one_hot_rows(ref, index_col, rows, strip):
    width = ref.shape[1]

    def body(i, _):
        at = pl.ds(pl.multiple_of(i * strip, strip), strip)
        lane = lax.broadcasted_iota(jnp.int32, (strip, width), 1)
        ref[at, :] = jnp.where(index_col[at, :] == lane, 1.0, 0.0).astype(jnp.bfloat16)
        return 0

    lax.fori_loop(0, rows // strip, body, 0)


def one_hot_cols(ref, index_row, rows, strip):
    width = ref.shape[1]

    def body(i, _):
        at = pl.ds(pl.multiple_of(i * strip, strip), strip)
        sub = lax.broadcasted_iota(jnp.int32, (strip, width), 0) + i * strip
        ref[at, :] = jnp.where(index_row[...] == sub, 1.0, 0.0).astype(jnp.bfloat16)
        return 0

    lax.fori_loop(0, rows // strip, body, 0)


def copy_to(src, dst, sems, at, **where):
    send, recv = sems
    return pltpu.make_async_remote_copy(
        src_ref=src,
        dst_ref=dst,
        send_sem=send.at[at],
        recv_sem=recv.at[at],
        device_id=where,
        device_id_type=pl.DeviceIdType.MESH,
    )


def group_kernel(
    owners,
    match,
    diag_own,
    tiles,
    trow,
    tcol,
    rel_row,
    rel_peer,
    rel_slot,
    rel_weight,
    pheno,
    x_out,
    r_out,
    imeta,
    fmeta,
    pairs,
    imeta_all,
    fmeta_all,
    tiles_all,
    ph_all,
    inv_v,
    inv,
    match_row,
    col_row,
    row_row,
    col_col,
    row_col,
    weight,
    diag,
    khi,
    klo,
    kthi,
    ktlo,
    pm,
    c,
    ct,
    rsel,
    rselt,
    d,
    r,
    xs,
    got,
    al,
    al_all,
    dcat,
    ycat,
    hcat,
    meta_send,
    meta_recv,
    tile_send,
    tile_recv,
    ph_send,
    ph_recv,
    out_send,
    out_recv,
    local_sem,
):
    persons = pheno.shape[0]
    every = owners * persons
    entries = c.shape[0]
    eown = entries // owners
    n = r.shape[1]
    held = pairs.shape[0]
    share = held // 2
    half = persons // 2
    nblk = persons // 64
    lists = 2 * owners
    blank = lists * held
    f = lax.axis_index("fam")
    t = lax.axis_index("trait")
    rep = lax.axis_index("rep")
    other = 1 - rep
    across = 1 - t
    me = f * 2 + rep
    peers = [lax.rem(f + k, owners) for k in range(1, owners)]
    sources = [lax.rem(f + owners - k, owners) for k in range(1, owners)]

    barrier = pltpu.get_barrier_semaphore()
    greet = [dict(fam=p, rep=q) for p in peers for q in (rep, other)]
    greet += [dict(rep=other), dict(trait=across)]
    for g in greet:
        pl.semaphore_signal(barrier, inc=1, device_id=g, device_id_type=pl.DeviceIdType.MESH)

    inner = rel_row[...] % 64
    imeta[...] = jnp.full(imeta.shape, -1, jnp.int32)
    fmeta[...] = jnp.zeros(fmeta.shape, jnp.float32)
    imeta[0 : persons // n, :] = match[...]
    imeta[4:5, :] = rel_peer[...] * persons + rel_slot[...]
    imeta[5:6, :] = rel_row[...] - inner + (inner % 2) * 32 + inner // 2
    imeta[6:7, 0:held] = trow[...] * nblk + tcol[...]
    fmeta[0 : persons // n, :] = diag_own[...]
    fmeta[4:5, :] = rel_weight[...]
    for i in range(32):
        pairs[:, i, :] = tiles[:, i * 128 : (i + 1) * 128]
    pl.semaphore_wait(barrier, len(greet))

    meta_sems = (meta_send, meta_recv)
    meta_copies = []
    at = 0
    for own, all_ in ((imeta, imeta_all), (fmeta, fmeta_all)):
        for g in greet[:-1]:
            cp = copy_to(own, all_.at[me], meta_sems, at, **g)
            cp.start()
            meta_copies.append(cp)
            at += 1

    def tiles_of(source, who, part):
        first = (source * 2 + who) * held + part * share
        return tiles_all.at[pl.ds(first, share)]

    tile_sems = (tile_send, tile_recv)
    k3 = owners - 1
    along = []
    for k, p in enumerate(peers):
        cp = copy_to(pairs.at[pl.ds(t * share, share)], tiles_of(f, rep, t), tile_sems, k, fam=p)
        cp.start()
        along.append(cp)
    own_tiles = tiles_all.at[pl.ds(me * held, held)]
    tile_home = copy_to(pairs, own_tiles, tile_sems, 4 * k3, rep=other)
    tile_home.start()

    keep = [
        pltpu.make_async_copy(imeta, imeta_all.at[me], local_sem.at[0]),
        pltpu.make_async_copy(fmeta, fmeta_all.at[me], local_sem.at[1]),
        pltpu.make_async_copy(pairs, own_tiles, local_sem.at[2]),
        pltpu.make_async_copy(
            pheno.at[:, pl.ds(pl.multiple_of(f * n, n), n)],
            ph_all.at[pl.ds(f * persons, persons)],
            local_sem.at[3],
        ),
    ]
    for cp in keep:
        cp.start()
    tiles_all[blank] = jnp.zeros(tiles_all.shape[1:], jnp.float32)
    for cp in keep:
        cp.wait()
    for cp in meta_copies:
        cp.wait()

    inv_v[...] = jnp.zeros(inv_v.shape, jnp.int32)
    pos_lane = lax.broadcasted_iota(jnp.int32, (held, n), 1)
    tile_id = lax.broadcasted_iota(jnp.int32, (held, n), 0)
    for o in range(owners):
        found = jnp.zeros((1, n), jnp.int32)
        for q in range(2):
            j = 2 * o + q
            im = imeta_all[j]
            imt = im.T
            at = slice(j * n, (j + 1) * n)
            col_row[:, at] = im[4:5]
            row_row[:, at] = im[5:6]
            col_col[at, :] = imt[:, 4:5]
            row_col[at, :] = imt[:, 5:6]
            fmt = fmeta_all[j].T
            weight[at, :] = fmt[:, 4:5]
            hit = jnp.where(imt[:held, 6:7] == pos_lane, tile_id + (j * held + 1), 0)
            found = jnp.maximum(found, jnp.max(hit, axis=0, keepdims=True))
            if q == 0:
                for i in range(persons // n):
                    at = slice(o * persons + i * n, o * persons + (i + 1) * n)
                    match_row[:, at] = im[i : i + 1]
                    diag[at, :] = fmt[:, i : i + 1]
        inv_v[o : o + 1, :] = jnp.where(found == 0, blank, found - 1)
    to_scalar = pltpu.make_async_copy(inv_v, inv, local_sem.at[4])
    to_scalar.start()

    tile_across, tile_side = [], []
    for k, s in enumerate(sources):
        along[k].wait()
        cp = copy_to(tiles_of(s, rep, t), tiles_of(s, rep, t), tile_sems, k3 + k, trait=across)
        cp.start()
        tile_across.append(cp)
        cp = copy_to(tiles_of(s, rep, t), tiles_of(s, rep, t), tile_sems, 2 * k3 + k, rep=other)
        cp.start()
        tile_side.append(cp)
    ph_sems = (ph_send, ph_recv)
    ph_along = []
    for k, p in enumerate(peers):
        cp = copy_to(
            pheno.at[pl.ds(rep * half, half), pl.ds(pl.multiple_of(p * n, n), n)],
            ph_all.at[pl.ds(f * persons + rep * half, half)],
            ph_sems,
            k,
            fam=p,
        )
        cp.start()
        ph_along.append(cp)

    one_hot_rows(rsel, row_col, entries, 64)
    for o in range(owners):
        lane = row_row[:, o * eown : (o + 1) * eown]
        sub = lax.broadcasted_iota(jnp.int32, (persons, eown), 0)
        rselt[o] = jnp.where(lane == sub, 1.0, 0.0).astype(jnp.bfloat16)
    for k, s in enumerate(sources):
        tile_across[k].wait()
        part = tiles_of(s, rep, across)
        cp = copy_to(part, part, tile_sems, 3 * k3 + k, rep=other)
        cp.start()
        tile_side.append(cp)
    one_hot_rows(c, col_col, entries, 64)
    one_hot_cols(ct, col_row, every, 64)
    one_hot_cols(pm, match_row, every, 64)
    to_scalar.wait()
    tile_home.wait()
    for cp in tile_side:
        cp.wait()

    def factor(o, _):
        for a2 in range(nblk // 2):
            rows = []
            for a in (2 * a2, 2 * a2 + 1):
                got = [tiles_all[inv[o, a * nblk + b]] for b in range(nblk)]
                rows.append(jnp.concatenate([g[:, :64] for g in got], axis=1))
                rows.append(jnp.concatenate([g[:, 64:] for g in got], axis=1))
            full = jnp.concatenate(rows, axis=0)
            at = slice(a2 * 128, (a2 + 1) * 128)
            high = full.astype(jnp.bfloat16)
            khi[o, at, :] = high
            klo[o, at, :] = (full - high.astype(jnp.float32)).astype(jnp.bfloat16)
            full = full.T
            high = full.astype(jnp.bfloat16)
            kthi[o, :, at] = high
            ktlo[o, :, at] = (full - high.astype(jnp.float32)).astype(jnp.bfloat16)
        return 0

    lax.fori_loop(0, owners, factor, 0)

    ph_side = []
    for k, s in enumerate(sources):
        ph_along[k].wait()
        part = ph_all.at[pl.ds(s * persons + rep * half, half)]
        cp = copy_to(part, part, ph_sems, k3 + k, rep=other)
        cp.start()
        ph_side.append(cp)

    def person(o):
        return pl.ds(o * persons, persons) if isinstance(o, int) else pl.ds(pl.multiple_of(o * persons, persons), persons)

    def entry(o):
        return pl.ds(o * eown, eown) if isinstance(o, int) else pl.ds(pl.multiple_of(o * eown, eown), eown)

    zero = jnp.zeros((1, n), jnp.float32)

    def colsum(v):
        return jnp.sum(v, axis=0, keepdims=True)

    for cp in ph_side:
        cp.wait()
    ycat[...] = split_terms(ph_all[...])

    out_sems = (out_send, out_recv)

    def block(o):
        return pl.ds(pl.multiple_of(o * n, n), n)

    early = half // 2

    def rows_of(o, first, count):
        return pl.ds(pl.multiple_of(o * persons + rep * half + first, early), count)

    def give(src, first, count, dst, k, unit):
        part = src.at[rows_of(peers[k], first, count)]
        cp = copy_to(part, dst, out_sems, unit * k3 + k, fam=peers[k])
        cp.start()
        return cp

    def give_early(src, which):
        return [give(src, 0, early, got.at[which, :, block(f)], k, which) for k in range(k3)]

    def begin(o, carry):
        rr, dd = carry
        v = fold(mm(pm[person(o), :], ycat[...]))
        r[person(o), :] = v
        d[0, person(o), :] = v
        dcat[person(o), :] = split_terms(v)
        square = v * v
        return rr + colsum(square), dd + colsum(square * diag[person(o), :])

    rr, dd = lax.fori_loop(0, owners, begin, (zero, zero), unroll=True)
    given = []

    def forward():
        spread = []
        for o in range(owners):
            g = fold(mm(c[entry(o), :], dcat[...])) * weight[entry(o), :]
            spread.append(split_terms(g))
        yy = zero
        for o in range(owners):
            near = dcat[person(o), :]
            y = fold(mm(khi[o], near) + mm(rselt[o], spread[o]))
            y = y + mm(klo[o], near[:, :n])
            ycat[person(o), :] = split_terms(y)
            yy = yy + colsum(y * y)
        for o in range(owners):
            h = fold(mm(rsel[entry(o), :], ycat[person(o), :])) * weight[entry(o), :]
            hcat[entry(o), :] = split_terms(h)
        return yy

    def image(o, step):
        ys = ycat[person(o), :]
        back = fold(mm(kthi[o], ys) + mm(ct[person(o), :], hcat[...]))
        back = back + mm(ktlo[o], ys[:, :n])
        return diag[person(o), :] * d[step, person(o), :] + back

    for step in range(ITERS - 1):
        yy = forward()
        alpha = rr / (yy + dd)
        for o in range(owners):
            at = slice(o * persons, (o + 1) * persons)
            move = alpha * d[step, at, :]
            xs[at, :] = move if step == 0 else xs[at, :] + move
        if step == ITERS - 2:
            given += give_early(xs, 0)

        def descend(o, acc):
            left = r[person(o), :] - alpha * image(o, step)
            r[person(o), :] = left
            return acc + colsum(left * left)

        nxt = lax.fori_loop(0, owners, descend, zero, unroll=True)
        beta = nxt / rr
        rr = nxt

        def turn(o, acc):
            v = r[person(o), :] + beta * d[step, person(o), :]
            d[step + 1, person(o), :] = v
            dcat[person(o), :] = split_terms(v)
            return acc + colsum(v * v * diag[person(o), :])

        dd = lax.fori_loop(0, owners, turn, zero, unroll=True)

    last = ITERS - 1
    given += give_early(d.at[last], 1)
    yy = forward()
    alpha = rr / (yy + dd)
    al[0:1, :] = alpha
    for k in range(k3):
        cp = copy_to(al, al_all.at[f], out_sems, 2 * k3 + k, fam=peers[k])
        cp.start()
        given.append(cp)

    mine = pl.ds(rep * half, half)
    mine_early = pl.ds(rep * half, early)
    mine_late = pl.ds(rep * half + early, half - early)
    for k in range(k3):
        at = rows_of(peers[k], early, half - early)
        xs[at, :] = xs[at, :] + alpha * d[last, at, :]
        given.append(give(xs, early, half - early, x_out.at[mine_late, block(f)], k, 3))
    theirs = []
    for k in range(owners):
        o = peers[k] if k < k3 else f
        r[person(o), :] = r[person(o), :] - alpha * image(o, last)
        if k < k3:
            theirs.append(give(r, 0, half, r_out.at[mine, block(f)], k, 4))
    stay = pltpu.make_async_copy(
        r.at[pl.ds(f * persons, persons)], r_out.at[:, block(f)], local_sem.at[5]
    )
    stay.start()
    for cp in given:
        cp.wait()

    home = rows_of(f, 0, half)
    x_out[mine, block(f)] = xs[home, :] + alpha * d[last, home, :]
    for s in sources:
        x_out[mine_early, block(s)] = got[0, :, block(s)] + al_all[s, 0:1, :] * got[1, :, block(s)]
    base = 5 * k3
    side = [copy_to(x_out.at[mine], x_out.at[mine], out_sems, base, rep=other)]
    side[0].start()
    for i, cp in enumerate(theirs):
        cp.wait()
        part = r_out.at[mine, block(sources[i])]
        cp = copy_to(part, part, out_sems, base + 1 + i, rep=other)
        cp.start()
        side.append(cp)
    for cp in side + [stay]:
        cp.wait()


def local_group(
    pheno,
    match,
    diag_var,
    tiles,
    tile_row_family,
    tile_cols,
    rel_row,
    rel_peer,
    rel_slot,
    rel_weight,
):
    owners = lax.axis_size("fam")
    persons, columns = pheno.shape
    n = columns // owners
    held = tiles.shape[0]
    lists = 2 * owners
    every = owners * persons
    entries = lists * rel_row.shape[0]
    eown = entries // owners
    vmem = pl.BlockSpec(memory_space=pltpu.VMEM)
    bf, f32, i32 = jnp.bfloat16, jnp.float32, jnp.int32
    k3 = owners - 1
    dma = pltpu.SemaphoreType.DMA
    return pl.pallas_call(
        functools.partial(group_kernel, owners),
        out_shape=[jax.ShapeDtypeStruct((persons, columns), f32)] * 2,
        in_specs=[vmem] * 10,
        out_specs=[vmem] * 2,
        scratch_shapes=[
            pltpu.VMEM((8, n), i32),
            pltpu.VMEM((8, n), f32),
            pltpu.VMEM((held, 32, 128), f32),
            pltpu.VMEM((lists, 8, n), i32),
            pltpu.VMEM((lists, 8, n), f32),
            pltpu.VMEM((lists * held + 1, 32, 128), f32),
            pltpu.VMEM((every, n), f32),
            pltpu.VMEM((8, n), i32),
            pltpu.SMEM((8, n), i32),
            pltpu.VMEM((1, every), i32),
            pltpu.VMEM((1, entries), i32),
            pltpu.VMEM((1, entries), i32),
            pltpu.VMEM((entries, 1), i32),
            pltpu.VMEM((entries, 1), i32),
            pltpu.VMEM((entries, 1), f32),
            pltpu.VMEM((every, 1), f32),
            pltpu.VMEM((owners, persons, persons), bf),
            pltpu.VMEM((owners, persons, persons), bf),
            pltpu.VMEM((owners, persons, persons), bf),
            pltpu.VMEM((owners, persons, persons), bf),
            pltpu.VMEM((every, every), bf),
            pltpu.VMEM((entries, every), bf),
            pltpu.VMEM((every, entries), bf),
            pltpu.VMEM((entries, persons), bf),
            pltpu.VMEM((owners, persons, eown), bf),
            pltpu.VMEM((ITERS, every, n), f32),
            pltpu.VMEM((every, n), f32),
            pltpu.VMEM((every, n), f32),
            pltpu.VMEM((2, persons // 4, columns), f32),
            pltpu.VMEM((8, n), f32),
            pltpu.VMEM((owners, 8, n), f32),
            pltpu.VMEM((every, 2 * n), bf),
            pltpu.VMEM((every, 2 * n), bf),
            pltpu.VMEM((entries, 2 * n), bf),
            dma((2 * lists - 2,)),
            dma((2 * lists - 2,)),
            dma((4 * k3 + 1,)),
            dma((4 * k3 + 1,)),
            dma((2 * k3,)),
            dma((2 * k3,)),
            dma((6 * k3 + 1,)),
            dma((6 * k3 + 1,)),
            dma((7,)),
        ],
        compiler_params=pltpu.CompilerParams(
            vmem_limit_bytes=60 * 2**20, collective_id=0, has_side_effects=True
        ),
    )(
        match.reshape(-1, n),
        diag_var.reshape(-1, n),
        tiles,
        tile_row_family.reshape(1, -1),
        tile_cols.reshape(1, -1),
        rel_row.reshape(1, -1),
        rel_peer.reshape(1, -1),
        rel_slot.reshape(1, -1),
        rel_weight.reshape(1, -1),
        pheno,
    )


def solution(mesh):
    placed = (
        P(("groups", "fam"), "trait"),
        P(("groups", "fam")),
        P(("groups", "fam")),
        P(("groups", "fam", "rep"), None),
        P(("groups", "fam", "rep")),
        P(("groups", "fam", "rep")),
        P(("groups", "fam", "rep")),
        P(("groups", "fam", "rep"), None),
        P(("groups", "fam", "rep")),
        P(("groups", "fam", "rep")),
    )
    whole = mesh.shape["fam"] == 4 and mesh.shape["trait"] == 2 and mesh.shape["rep"] == 2
    return jax.shard_map(
        local_group if whole else local,
        mesh=mesh,
        in_specs=placed,
        out_specs=(P(("groups", "fam"), "trait"), P(("groups", "fam"), "trait")),
        check_vma=False,
    )
```
